256 devices in a mesh: seq: 32 (over y, x, core), fsdp: 8 (over z).
Axes of the slice: x: 4, y: 4, z: 8, core: 2. Of those that a mesh axis runs over, the one named last changes fastest.
Arguments:
- self_q: bfloat16 [8, 4096, 4096], P('fsdp', 'seq'), may hold values from -128 to 128
- self_k: bfloat16 [8, 4096, 4096], P('fsdp', 'seq'), may hold values from -32 to 32
- self_v: bfloat16 [8, 4096, 4096], P('fsdp', 'seq'), may hold values from -6 to 6
- cross_q: bfloat16 [8, 4096, 4096], P('fsdp', 'seq'), may hold values from -160 to 160
- audio: bfloat16 [8, 1024, 768], P('fsdp', 'seq'), may hold values from -6 to 6
- key_weight: bfloat16 [768, 4096], P('fsdp', 'seq'), may hold values from -0.21875 to 0.21875
- value_weight: bfloat16 [768, 4096], P('fsdp', 'seq'), may hold values from -0.21875 to 0.21875
- intersection: int32 [8, 64, 4], P('fsdp', 'seq'), may hold values from 0 to 63, as said below
- counts: int32 [8, 64], P('fsdp', 'seq'), may hold values from 1 to 4, as said below
- cotangent: bfloat16 [8, 4096, 4096], P('fsdp', 'seq'), may hold values from -6 to 6
Outputs:
- block_out: bfloat16 [8, 4096, 4096], P('fsdp', 'seq')
- audio_grad: float32 [8, 1024, 768], P('fsdp', 'seq')
The draws below stay inside these ranges and needn't reach their ends.
Inputs may be any that keep to these rules, and one draw needn't show every extreme that they name: `intersection`: the first counts entries of a frame's list are distinct consecutive blocks, each within 3 blocks of block f for frame f; later entries are padding and are ignored. `counts`: every clip has a frame whose window holds 4 blocks.
All inputs are finite; a program needn't handle non-finite values.
Results may differ from the reference program's by a relative error of at most 0.015.
The reference program's roundings to bfloat16 on the way count: a program that leaves them out, or rounds other values in their place, can miss the bound.
Values may be sent and summed in bfloat16 or wider, within the bound.
No kernel may reach another device: no remote copies, remote signals or barrier semaphores. Data moves between devices by JAX's collectives and lax.ppermute only.
A program may use at most 128 MiB of HBM per device.

```python
import jax
import jax.numpy as jnp
from jax import lax

HD = 128
A = 768
HEADS = 32
FRAME_TOK = 64
LENGTH = 4096
FRAMES = 64
AB = 16
BLOCKS = 64
AUDIO = 1024
MAXB = 4
WIN = 64
CLIPS = 8


def attention_bases(key):
    shape = (CLIPS, LENGTH, HEADS * HD)
    base_q = jnp.clip(jax.random.normal(jax.random.fold_in(key, 101), shape, jnp.float32), -6.0, 6.0)
    base_k = jnp.clip(jax.random.normal(jax.random.fold_in(key, 102), shape, jnp.float32), -6.0, 6.0)
    return (base_q, base_k)


def draw_self_q(key, part):
    base_q, base_k = attention_bases(key)
    return base_q.astype(jnp.bfloat16)


def draw_self_k(key, part):
    base_q, base_k = attention_bases(key)
    return base_k.astype(jnp.bfloat16)


def draw_cross_q(key, part):
    key = jax.random.fold_in(key, 3)
    shape = (CLIPS, LENGTH, HEADS * HD)
    base = jnp.clip(jax.random.normal(key, shape, jnp.float32), -6.0, 6.0)
    return base.astype(jnp.bfloat16)


def window_lists(key):
    first = jax.random.fold_in(key, 201)
    second = jax.random.fold_in(key, 202)
    third = jax.random.fold_in(key, 203)
    fourth = jax.random.fold_in(key, 204)
    sizes = jax.random.randint(first, (CLIPS, FRAMES), 1, MAXB + 1, dtype=jnp.int32)
    chosen = jax.random.randint(second, (CLIPS,), 0, FRAMES, dtype=jnp.int32)
    frame_index = jnp.arange(FRAMES, dtype=jnp.int32)
    sizes = jnp.where(frame_index[None, :] == chosen[:, None], MAXB, sizes)
    center = frame_index * BLOCKS // FRAMES
    jitter = jax.random.randint(third, (CLIPS, FRAMES), -1, 2, dtype=jnp.int32)
    start = jnp.clip(center[None, :] + jitter - sizes // 2, 0, BLOCKS - sizes)
    slots = jnp.arange(MAXB, dtype=jnp.int32)
    live_ids = start[:, :, None] + slots[None, None, :]
    padding = jax.random.randint(fourth, (CLIPS, FRAMES, MAXB), 0, BLOCKS, dtype=jnp.int32)
    window_ids = jnp.where(slots[None, None, :] < sizes[:, :, None], live_ids, padding)
    return (window_ids, sizes)


def draw_intersection(key, part):
    window_ids, sizes = window_lists(key)
    return window_ids


def draw_counts(key, part):
    window_ids, sizes = window_lists(key)
    return sizes


def steps_of(own_key, extent, shards, low, high):
    def one(dim, blocks):
        heights = jax.random.uniform(jax.random.fold_in(jax.random.fold_in(own_key, 6), dim), (blocks,), jnp.float32, low / len(shards), high / len(shards))
        return jnp.repeat(jnp.exp(heights), extent[dim] // blocks).reshape((-1,) + (1,) * (len(extent) - dim - 1))

    factor_of = one(*shards[0])
    for cut in shards[1:]:
        factor_of = factor_of * one(*cut)
    return factor_of


def gaussian(own_key, shape, spread, limit, cuts=(), kind=jnp.bfloat16):
    array = spread * jax.random.normal(own_key, shape, jnp.float32)
    if cuts:
        array = array * steps_of(own_key, shape, cuts, -0.22, 0.18)
    return jnp.clip(array, -limit, limit).astype(kind)


def setup_inputs(seed: int = 0) -> dict:
    key_list = jax.random.split(jax.random.key(seed), 11)
    self_q = draw_self_q(jax.random.fold_in(key_list[10], 71), 0)
    self_k = draw_self_k(jax.random.fold_in(key_list[10], 71), 0)
    self_v = gaussian(key_list[2], (CLIPS, LENGTH, HEADS * HD), 1.0, 6.0, ((0, 8), (1, 32)))
    cross_q = draw_cross_q(jax.random.fold_in(key_list[10], 71), 0)
    audio = gaussian(key_list[4], (CLIPS, AUDIO, A), 1.0, 6.0, ((0, 8), (1, 32)))
    key_weight = gaussian(key_list[5], (A, HEADS * HD), A ** -0.5, 0.21875, ((0, 8), (1, 32)))
    value_weight = gaussian(key_list[6], (A, HEADS * HD), A ** -0.5, 0.21875, ((0, 8), (1, 32)))
    intersection = draw_intersection(jax.random.fold_in(key_list[10], 71), 0)
    counts = draw_counts(jax.random.fold_in(key_list[10], 71), 0)
    cotangent = gaussian(key_list[9], (CLIPS, LENGTH, HEADS * HD), 1.0, 6.0, ((0, 8), (1, 32)))
    return {"self_q": self_q, "self_k": self_k, "self_v": self_v, "cross_q": cross_q, "audio": audio, "key_weight": key_weight, "value_weight": value_weight, "intersection": intersection, "counts": counts, "cotangent": cotangent}


def self_attention(q_clip, k_clip, v_clip):
    length = q_clip.shape[0]
    scaling = HD ** -0.5

    def split_heads(matrix):
        return matrix.reshape(length, HEADS, HD).transpose(1, 0, 2)

    def one_head(pieces):
        queries, key_rows, value_rows = pieces
        scores = jnp.dot(queries, key_rows.T, preferred_element_type=jnp.float32) * scaling
        highest = jnp.max(scores, axis=1, keepdims=True)
        raised = jnp.exp(scores - highest)
        weights = (raised / jnp.sum(raised, axis=1, keepdims=True)).astype(jnp.bfloat16)
        return jnp.dot(weights, value_rows, preferred_element_type=jnp.float32).astype(jnp.bfloat16)

    outputs = lax.map(one_head, (split_heads(q_clip), split_heads(k_clip), split_heads(v_clip)))
    return outputs.transpose(1, 0, 2).reshape(length, HEADS * HD)


def window_rows(window_ids):
    offsets = jnp.arange(AB, dtype=jnp.int32)
    return (window_ids[:, :, None] * AB + offsets[None, None, :]).reshape(window_ids.shape[0], MAXB * AB)


def audio_attention(queries, grad_rows, key_slots, value_slots, live_counts):
    f32 = jnp.float32
    scaling = HD ** -0.5
    slots = key_slots.shape[1]
    live_slots = (jnp.arange(slots, dtype=jnp.int32) // AB)[None, :] < live_counts[:, None]
    scores = jnp.einsum("ftha,fwha->fhtw", queries.astype(f32), key_slots.astype(f32)) * scaling
    scores = jnp.where(live_slots[:, None, None, :], scores, -1e30)
    highest = jnp.max(scores, axis=3, keepdims=True)
    raised = jnp.exp(scores - highest)
    weights = raised / jnp.sum(raised, axis=3, keepdims=True)
    weights_b = weights.astype(jnp.bfloat16)
    mixed = jnp.einsum("fhtw,fwha->ftha", weights_b.astype(f32), value_slots.astype(f32))
    d_values = jnp.einsum("fhtw,ftha->fwha", weights_b.astype(f32), grad_rows.astype(f32)).astype(jnp.bfloat16)
    d_probs = jnp.einsum("ftha,fwha->fhtw", grad_rows.astype(f32), value_slots.astype(f32))
    d_scores = (weights * (d_probs - jnp.sum(weights * d_probs, axis=3, keepdims=True))).astype(jnp.bfloat16)
    d_keys = (jnp.einsum("fhtw,ftha->fwha", d_scores.astype(f32), queries.astype(f32)) * scaling).astype(jnp.bfloat16)
    return mixed, d_keys, d_values


def reference(self_q, self_k, self_v, cross_q, audio, key_weight, value_weight, intersection, counts, cotangent):
    block_list = []
    grad_list = []
    for clip_index in range(CLIPS):
        own = self_attention(self_q[clip_index], self_k[clip_index], self_v[clip_index])
        key_rows = jnp.dot(audio[clip_index], key_weight, preferred_element_type=jnp.float32).astype(jnp.bfloat16)
        value_rows = jnp.dot(audio[clip_index], value_weight, preferred_element_type=jnp.float32).astype(jnp.bfloat16)
        slot_rows = window_rows(intersection[clip_index])
        key_slots = key_rows[slot_rows].reshape(FRAMES, WIN, HEADS, HD)
        value_slots = value_rows[slot_rows].reshape(FRAMES, WIN, HEADS, HD)
        queries = cross_q[clip_index].reshape(FRAMES, FRAME_TOK, HEADS, HD)
        grad_rows = cotangent[clip_index].reshape(FRAMES, FRAME_TOK, HEADS, HD)
        mixed, d_keys, d_values = audio_attention(queries, grad_rows, key_slots, value_slots, counts[clip_index])
        block = (own.astype(jnp.float32) + mixed.reshape(LENGTH, HEADS * HD)).astype(jnp.bfloat16)
        slot_grads = jnp.dot(d_keys.reshape(FRAMES * WIN, HEADS * HD), key_weight.T, preferred_element_type=jnp.float32)
        slot_grads = slot_grads + jnp.dot(d_values.reshape(FRAMES * WIN, HEADS * HD), value_weight.T, preferred_element_type=jnp.float32)
        grad_clip = jax.ops.segment_sum(slot_grads, slot_rows.reshape(-1), num_segments=AUDIO)
        block_list.append(block)
        grad_list.append(grad_clip)
    return jnp.stack(block_list), jnp.stack(grad_list)
```

```python
import functools

import jax
import jax.numpy as jnp
from jax import lax
from jax.experimental import pallas as pl
from jax.experimental.pallas import tpu as pltpu
from jax.sharding import PartitionSpec as P

HD = 128
AB = 16
MAXB = 4
REACH = 3
SCALING = HD ** (-0.5)
EXP2_SCALING = SCALING * 1.4426950408889634
F32 = jnp.float32
BF16 = jnp.bfloat16
VMEM_BYTES = 48 * 1024 * 1024


def passed_along(block, axis, distance):
    devices = range(lax.axis_size(axis))
    route = [(i - distance, i) for i in devices if i - distance in devices]
    return lax.ppermute(block, axis, route)


def gathered_by_doubling(block, axis):
    size = lax.axis_size(axis)
    here = lax.axis_index(axis)
    step = 1
    while step < size:
        other = lax.ppermute(block, axis, [(i, i ^ step) for i in range(size)])
        upper = (here & step) != 0
        block = jnp.concatenate(
            [jnp.where(upper, other, block), jnp.where(upper, block, other)], axis=0
        )
        step *= 2
    return block


def heads_first_kernel(group, q_ref, k_ref, v_ref, out_ref):
    rows = q_ref.shape[0]
    for head in range(group):
        cols = slice(head * HD, (head + 1) * HD)
        out_ref[head, 0:rows] = q_ref[:, cols]
        out_ref[head, rows : 2 * rows] = k_ref[:, cols]
        out_ref[head, 2 * rows : 3 * rows] = v_ref[:, cols]


def heads_first(q_local, k_local, v_local):
    _, rows, width = q_local.shape
    heads = width // HD
    group = 8
    block = pl.BlockSpec((None, rows, group * HD), lambda i: (0, 0, i))
    return pl.pallas_call(
        functools.partial(heads_first_kernel, group),
        grid=(heads // group,),
        in_specs=[block] * 3,
        out_specs=pl.BlockSpec((group, 3 * rows, HD), lambda i: (i, 0, 0)),
        out_shape=jax.ShapeDtypeStruct((heads, 3 * rows, HD), BF16),
        compiler_params=pltpu.CompilerParams(vmem_limit_bytes=VMEM_BYTES),
        cost_estimate=pl.CostEstimate(
            flops=0, bytes_accessed=6 * rows * width * 2, transcendentals=0
        ),
        name="heads_first",
    )(q_local, k_local, v_local)


def self_attention_kernel(
    block_rows, block_keys, q_ref, k_ref, v_ref, out_ref, keys_t, values_x, scores, tops
):
    length = out_ref.shape[0]
    key_blocks = length // block_keys
    query_blocks = length // block_rows
    chunk = q_ref.shape[1]
    for piece in range(length // chunk):
        keys_t[:, piece * chunk : (piece + 1) * chunk] = k_ref[piece].T
        values_x[piece * chunk : (piece + 1) * chunk, :HD] = v_ref[piece]
    values_x[:, HD:] = jnp.ones((length, HD), BF16)
    per_block = block_rows // chunk

    def queries_of(block):
        rows = q_ref[pl.ds(block * per_block, per_block)]
        return rows.reshape(block_rows, HD)

    def highest(top, part):
        for group in range(part.shape[1] // HD):
            lanes = part[:, group * HD : (group + 1) * HD]
            top = lanes if top is None else jnp.maximum(top, lanes)
        return top

    def row_max(top):
        return jnp.broadcast_to(jnp.max(top, axis=1, keepdims=True), (block_rows, HD))

    first = queries_of(0)
    top = None
    for j in range(key_blocks):
        keys = slice(j * block_keys, (j + 1) * block_keys)
        part = jnp.dot(first, keys_t[:, keys], preferred_element_type=F32)
        scores[0, :, keys] = part
        top = highest(top, part)
    tops[0] = row_max(top)

    def body(i, carry):
        slot = lax.rem(i, 2)
        later = 1 - slot
        queries = queries_of(jnp.minimum(i + 1, query_blocks - 1))
        top_here = tops[slot][:, :1]
        top = None
        total = None
        for j in range(key_blocks):
            keys = slice(j * block_keys, (j + 1) * block_keys)
            part = jnp.dot(queries, keys_t[:, keys], preferred_element_type=F32)
            scores[later, :, keys] = part
            top = highest(top, part)
            raised = jnp.exp2((scores[slot, :, keys] - top_here) * EXP2_SCALING).astype(BF16)
            mixed = jnp.dot(raised, values_x[keys, :], preferred_element_type=F32)
            total = mixed if total is None else total + mixed
        tops[later] = row_max(top)
        rows = pl.ds(pl.multiple_of(i * block_rows, block_rows), block_rows)
        out_ref[rows, :] = (total[:, :HD] / total[:, HD:]).astype(BF16)
        return carry

    lax.fori_loop(0, query_blocks, body, 0)


def attend_self(qkv):
    sources, _, rows, _ = qkv.shape
    length = sources * rows
    block_rows, block_keys = 512, 512

    def part(which):
        return pl.BlockSpec((sources, None, rows, HD), lambda i: (0, which, 0, 0))

    return pl.pallas_call(
        functools.partial(self_attention_kernel, block_rows, block_keys),
        grid=(1,),
        in_specs=[part(0), part(1), part(2)],
        out_specs=pl.BlockSpec((length, HD), lambda i: (0, 0)),
        out_shape=jax.ShapeDtypeStruct((length, HD), BF16),
        scratch_shapes=[
            pltpu.VMEM((HD, length), BF16),
            pltpu.VMEM((length, 2 * HD), BF16),
            pltpu.VMEM((2, block_rows, length), F32),
            pltpu.VMEM((2, block_rows, HD), F32),
        ],
        compiler_params=pltpu.CompilerParams(vmem_limit_bytes=VMEM_BYTES),
        cost_estimate=pl.CostEstimate(
            flops=8 * length * length * HD,
            bytes_accessed=8 * length * HD,
            transcendentals=length * length,
        ),
        name="self_attention",
    )(qkv, qkv, qkv)


def contract(a, b, dim_a, dim_b):
    return lax.dot_general(a, b, (((dim_a,), (dim_b,)), ((), ())), preferred_element_type=F32)


def cross_kernel(
    group, near_ref, live_ref, proj_ref, q_ref, grad_ref, own_ref, out_ref, audio_grad_ref
):
    @pl.when(pl.program_id(0) == 0)
    def _():
        audio_grad_ref[...] = jnp.zeros_like(audio_grad_ref)

    near = near_ref[...]
    live = live_ref[...] > 0
    sent = None
    for head in range(group):
        cols = slice(head * HD, (head + 1) * HD)
        proj = proj_ref[head]
        both = jnp.dot(near, proj, preferred_element_type=F32).astype(BF16)
        keys = both[:, :HD]
        values = both[:, HD:]
        queries = q_ref[:, cols]
        grads = grad_ref[:, cols]
        scores = contract(queries, keys, 1, 1) * SCALING
        scores = jnp.where(live, scores, -1e30)
        raised = jnp.exp(scores - jnp.max(scores, axis=1, keepdims=True))
        weights = raised / jnp.sum(raised, axis=1, keepdims=True)
        weights_b = weights.astype(BF16)
        mixed = jnp.dot(weights_b, values, preferred_element_type=F32)
        out_ref[:, cols] = (own_ref[head].astype(F32) + mixed).astype(BF16)
        d_values = contract(weights_b, grads, 0, 0).astype(BF16)
        d_probs = contract(grads, values, 1, 1)
        weighed = weights * d_probs
        d_scores = (
            weighed - weights * jnp.sum(weighed, axis=1, keepdims=True)
        ).astype(BF16)
        d_keys = (contract(d_scores, queries, 0, 0) * SCALING).astype(BF16)
        d_both = jnp.concatenate([d_keys, d_values], axis=1)
        term = contract(d_both, proj, 1, 1)
        sent = term if sent is None else sent + term
    audio_grad_ref[...] += sent


def cross_attention(near, live, proj, queries, grads, own):
    heads, features, _ = proj.shape
    rows, width = queries.shape
    band = near.shape[0]
    group = 4
    return pl.pallas_call(
        functools.partial(cross_kernel, group),
        grid=(heads // group,),
        in_specs=[
            pl.BlockSpec((band, features), lambda i: (0, 0)),
            pl.BlockSpec((rows, band), lambda i: (0, 0)),
            pl.BlockSpec((group, features, 2 * HD), lambda i: (i, 0, 0)),
            pl.BlockSpec((rows, group * HD), lambda i: (0, i)),
            pl.BlockSpec((rows, group * HD), lambda i: (0, i)),
            pl.BlockSpec((group, rows, HD), lambda i: (i, 0, 0)),
        ],
        out_specs=[
            pl.BlockSpec((rows, group * HD), lambda i: (0, i)),
            pl.BlockSpec((band, features), lambda i: (0, 0)),
        ],
        out_shape=[
            jax.ShapeDtypeStruct((rows, width), BF16),
            jax.ShapeDtypeStruct((band, features), F32),
        ],
        compiler_params=pltpu.CompilerParams(vmem_limit_bytes=VMEM_BYTES),
        cost_estimate=pl.CostEstimate(
            flops=8 * band * features * 2 * width,
            bytes_accessed=proj.size * 2 + 8 * rows * width,
            transcendentals=rows * band * heads,
        ),
        name="cross_attention",
    )(near, live, proj, queries, grads, own)


def live_band(window_ids, live_counts, band_first, band_blocks, frame_rows):
    slots = jnp.arange(window_ids.shape[1], dtype=jnp.int32)
    blocks = band_first + jnp.arange(band_blocks, dtype=jnp.int32)
    hits = (window_ids[:, :, None] == blocks[None, None, :]) & (
        slots[None, :, None] < live_counts[:, None, None]
    )
    live = jnp.any(hits, axis=1).astype(F32)
    return jnp.repeat(jnp.repeat(live, AB, axis=1), frame_rows, axis=0)


def local(
    self_q,
    self_k,
    self_v,
    cross_q,
    audio,
    key_weight,
    value_weight,
    intersection,
    counts,
    cotangent,
):
    both = jnp.concatenate([key_weight, value_weight], axis=1)
    cols = gathered_by_doubling(both[None], "fsdp")
    cols = cols.reshape(1, -1, 2 * HD)
    proj = lax.all_gather(cols, "seq", axis=0, tiled=True)

    rows = self_q.shape[1]
    qkv = heads_first(self_q, self_k, self_v)
    qkv = lax.all_to_all(qkv, "seq", split_axis=0, concat_axis=0, tiled=True)
    qkv = qkv.reshape(qkv.shape[0], 3, rows, HD)
    own_heads = attend_self(qkv)
    own_heads = own_heads.reshape(-1, rows, HD)
    own_tokens = lax.all_to_all(own_heads, "seq", split_axis=0, concat_axis=0, tiled=True)

    owned = audio.shape[1]
    half = owned // 2
    here = lax.axis_index("seq")
    frames = intersection.shape[1]
    mine = audio[0]
    near = jnp.concatenate(
        [
            passed_along(mine[half:], "seq", 2),
            passed_along(mine, "seq", 1),
            mine,
            passed_along(mine, "seq", -1),
            passed_along(mine[:half], "seq", -2),
        ],
        axis=0,
    )
    band_blocks = near.shape[0] // AB
    band_first = here * (owned // AB) - REACH
    live = live_band(intersection[0], counts[0], band_first, band_blocks, rows // frames)
    block_out, band = cross_attention(
        near, live, proj, cross_q[0], cotangent[0], own_tokens
    )

    total = band[half + owned : half + 2 * owned]
    band_b = band.astype(BF16)
    before = passed_along(band_b[half : half + owned], "seq", -1)
    after = passed_along(band_b[half + 2 * owned : half + 3 * owned], "seq", 1)
    far_before = passed_along(band_b[:half], "seq", -2)
    far_after = passed_along(band_b[half + 3 * owned :], "seq", 2)
    far = jnp.concatenate([far_after, far_before], axis=0)
    total = total + before.astype(F32) + after.astype(F32) + far.astype(F32)
    return (block_out[None], total[None])


def solution(mesh):
    in_specs = (
        P("fsdp", "seq", None),
        P("fsdp", "seq", None),
        P("fsdp", "seq", None),
        P("fsdp", "seq", None),
        P("fsdp", "seq", None),
        P("fsdp", "seq"),
        P("fsdp", "seq"),
        P("fsdp", "seq", None),
        P("fsdp", "seq"),
        P("fsdp", "seq", None),
    )
    out_specs = (P("fsdp", "seq", None), P("fsdp", "seq", None))
    return jax.shard_map(local, mesh=mesh, in_specs=in_specs, out_specs=out_specs, check_vma=False)
```

```python
import functools

import jax
import jax.numpy as jnp
from jax import lax
from jax.experimental import pallas as pl
from jax.experimental.pallas import tpu as pltpu
from jax.sharding import PartitionSpec as P

HD = 128
AB = 16
MAXB = 4
REACH = 3
SCALING = HD ** (-0.5)
EXP2_SCALING = SCALING * 1.4426950408889634
F32 = jnp.float32
BF16 = jnp.bfloat16
VMEM_BYTES = 48 * 1024 * 1024
CROSS_GROUP = 8


def passed_along(block, axis, distance):
    devices = range(lax.axis_size(axis))
    route = [(i - distance, i) for i in devices if i - distance in devices]
    return lax.ppermute(block, axis, route)


def round_ring(block, axis, distance):
    size = lax.axis_size(axis)
    return lax.ppermute(block, axis, [(i, (i + distance) % size) for i in range(size)])


def from_other_core(block):
    size = lax.axis_size("seq")
    return lax.ppermute(block, "seq", [(i, i ^ 1) for i in range(size)])


def heads_first_kernel(group, q_ref, k_ref, v_ref, out_ref):
    rows = q_ref.shape[0]
    for head in range(group):
        cols = slice(head * HD, (head + 1) * HD)
        out_ref[head, 0:rows] = q_ref[:, cols]
        out_ref[head, rows : 2 * rows] = k_ref[:, cols]
        out_ref[head, 2 * rows : 3 * rows] = v_ref[:, cols]


def heads_first(q_local, k_local, v_local):
    _, rows, width = q_local.shape
    heads = width // HD
    group = 8
    block = pl.BlockSpec((None, rows, group * HD), lambda i: (0, 0, i))
    return pl.pallas_call(
        functools.partial(heads_first_kernel, group),
        grid=(heads // group,),
        in_specs=[block] * 3,
        out_specs=pl.BlockSpec((group, 3 * rows, HD), lambda i: (i, 0, 0)),
        out_shape=jax.ShapeDtypeStruct((heads, 3 * rows, HD), BF16),
        compiler_params=pltpu.CompilerParams(vmem_limit_bytes=VMEM_BYTES),
        cost_estimate=pl.CostEstimate(
            flops=0, bytes_accessed=6 * rows * width * 2, transcendentals=0
        ),
        name="heads_first",
    )(q_local, k_local, v_local)


def self_attention_kernel(block_rows, block_keys, operands, *refs):
    q_ref, k_ref, v_ref = refs[:3]
    out_ref, keys_t, values_x, scores, tops = refs[operands:]
    chunk = q_ref.shape[1]
    length = k_ref.shape[0] * chunk
    key_blocks = length // block_keys
    query_blocks = out_ref.shape[0] // block_rows
    for piece in range(length // chunk):
        keys_t[:, piece * chunk : (piece + 1) * chunk] = k_ref[piece].T
        values_x[piece * chunk : (piece + 1) * chunk, :HD] = v_ref[piece]
    values_x[:, HD:] = jnp.ones((length, HD), BF16)
    per_block = block_rows // chunk

    def queries_of(block):
        rows = q_ref[pl.ds(block * per_block, per_block)]
        return rows.reshape(block_rows, HD)

    def highest(top, part):
        for group in range(part.shape[1] // HD):
            lanes = part[:, group * HD : (group + 1) * HD]
            top = lanes if top is None else jnp.maximum(top, lanes)
        return top

    def row_max(top):
        return jnp.broadcast_to(jnp.max(top, axis=1, keepdims=True), (block_rows, HD))

    first = queries_of(0)
    top = None
    for j in range(key_blocks):
        keys = slice(j * block_keys, (j + 1) * block_keys)
        part = jnp.dot(first, keys_t[:, keys], preferred_element_type=F32)
        scores[0, :, keys] = part
        top = highest(top, part)
    tops[0] = row_max(top)

    def body(i, carry):
        slot = lax.rem(i, 2)
        later = 1 - slot
        queries = queries_of(jnp.minimum(i + 1, query_blocks - 1))
        top_here = tops[slot][:, :1]
        top = None
        total = None
        for j in range(key_blocks):
            keys = slice(j * block_keys, (j + 1) * block_keys)
            part = jnp.dot(queries, keys_t[:, keys], preferred_element_type=F32)
            scores[later, :, keys] = part
            top = highest(top, part)
            raised = jnp.exp2((scores[slot, :, keys] - top_here) * EXP2_SCALING).astype(BF16)
            mixed = jnp.dot(raised, values_x[keys, :], preferred_element_type=F32)
            total = mixed if total is None else total + mixed
        tops[later] = row_max(top)
        rows = pl.ds(pl.multiple_of(i * block_rows, block_rows), block_rows)
        out_ref[rows, :] = (total[:, :HD] / total[:, HD:]).astype(BF16)
        return carry

    lax.fori_loop(0, query_blocks, body, 0)


def attend_self(qkv, part, parts, so_far=None):
    sources, _, rows, _ = qkv.shape
    length = sources * rows
    block_rows, block_keys = 512, 512
    q_sources = sources // parts

    def whole(which):
        return pl.BlockSpec((sources, None, rows, HD), lambda i: (0, which, 0, 0))

    operands = [qkv, qkv, qkv]
    in_specs = [
        pl.BlockSpec((q_sources, None, rows, HD), lambda i: (part, 0, 0, 0)),
        whole(1),
        whole(2),
    ]
    aliases = {}
    if so_far is not None:
        operands.append(so_far)
        in_specs.append(pl.BlockSpec(memory_space=pl.ANY))
        aliases = {3: 0}
    return pl.pallas_call(
        functools.partial(self_attention_kernel, block_rows, block_keys, len(operands)),
        grid=(1,),
        in_specs=in_specs,
        out_specs=pl.BlockSpec((length // parts, HD), lambda i: (part, 0)),
        out_shape=jax.ShapeDtypeStruct((length, HD), BF16),
        scratch_shapes=[
            pltpu.VMEM((HD, length), BF16),
            pltpu.VMEM((length, 2 * HD), BF16),
            pltpu.VMEM((2, block_rows, length), F32),
            pltpu.VMEM((2, block_rows, HD), F32),
        ],
        input_output_aliases=aliases,
        compiler_params=pltpu.CompilerParams(vmem_limit_bytes=VMEM_BYTES),
        cost_estimate=pl.CostEstimate(
            flops=8 * length * length * HD // parts,
            bytes_accessed=8 * length * HD,
            transcendentals=length * length // parts,
        ),
        name="self_attention",
    )(*operands)


def contract(a, b, dim_a, dim_b):
    return lax.dot_general(a, b, (((dim_a,), (dim_b,)), ((), ())), preferred_element_type=F32)


def cross_kernel(
    group,
    pieces,
    place_ref,
    near_ref,
    live_ref,
    q_ref,
    grad_ref,
    *refs,
):
    proj_refs = refs[: 2 * pieces]
    out_ref, audio_grad_ref, proj = refs[2 * pieces :]

    @pl.when(pl.program_id(0) == 0)
    def _():
        audio_grad_ref[...] = jnp.zeros_like(audio_grad_ref)

    depth = proj_refs[0].shape[1]
    for kind in range(2):
        lanes = pl.ds(pl.multiple_of(place_ref[pieces + kind], HD), HD)
        for piece in range(pieces):
            rows = pl.ds(pl.multiple_of(place_ref[piece], 32), depth)
            proj[:, rows, lanes] = proj_refs[kind * pieces + piece][...]

    near = near_ref[...]
    live = live_ref[...] > 0
    heads = range(group)
    cols = [slice(head * HD, (head + 1) * HD) for head in heads]
    both = [
        jnp.dot(near, proj[head], preferred_element_type=F32).astype(BF16) for head in heads
    ]
    keys = [part[:, :HD] for part in both]
    values = [part[:, HD:] for part in both]
    scores = [contract(q_ref[:, cols[head]], keys[head], 1, 1) for head in heads]
    d_probs = [contract(grad_ref[:, cols[head]], values[head], 1, 1) for head in heads]
    weights = []
    for head in heads:
        masked = jnp.where(live, scores[head], -1e30)
        top = jnp.max(masked, axis=1, keepdims=True)
        raised = jnp.exp2((masked - top) * EXP2_SCALING)
        weights.append(raised / jnp.sum(raised, axis=1, keepdims=True))
    weights_b = [part.astype(BF16) for part in weights]
    d_scores = []
    for head in heads:
        weighed = weights[head] * d_probs[head]
        inner = jnp.sum(weighed, axis=1, keepdims=True)
        d_scores.append((weighed - weights[head] * inner).astype(BF16))
    for head in heads:
        out_ref[:, cols[head]] = jnp.dot(
            weights_b[head], values[head], preferred_element_type=F32
        )
    d_values = [
        contract(weights_b[head], grad_ref[:, cols[head]], 0, 0).astype(BF16) for head in heads
    ]
    d_keys = [
        (contract(d_scores[head], q_ref[:, cols[head]], 0, 0) * SCALING).astype(BF16)
        for head in heads
    ]
    sent = None
    for head in heads:
        d_both = jnp.concatenate([d_keys[head], d_values[head]], axis=1)
        term = contract(d_both, proj[head], 1, 1)
        sent = term if sent is None else sent + term
    audio_grad_ref[...] += sent


def cross_attention(place, near, live, queries, grads, own_pieces, other_pieces):
    heads, depth, _ = own_pieces[0].shape
    pieces = len(own_pieces)
    features = depth * pieces
    rows, width = queries.shape
    band = near.shape[0]
    group = CROSS_GROUP
    piece = pl.BlockSpec((group, depth, HD), lambda i: (i, 0, 0))
    return pl.pallas_call(
        functools.partial(cross_kernel, group, pieces),
        grid=(heads // group,),
        in_specs=[
            pl.BlockSpec(memory_space=pltpu.SMEM),
            pl.BlockSpec((band, features), lambda i: (0, 0)),
            pl.BlockSpec((rows, band), lambda i: (0, 0)),
            pl.BlockSpec((rows, group * HD), lambda i: (0, i)),
            pl.BlockSpec((rows, group * HD), lambda i: (0, i)),
        ]
        + [piece] * (2 * pieces),
        out_specs=[
            pl.BlockSpec((rows, group * HD), lambda i: (0, i)),
            pl.BlockSpec((band, features), lambda i: (0, 0)),
        ],
        out_shape=[
            jax.ShapeDtypeStruct((rows, width), F32),
            jax.ShapeDtypeStruct((band, features), F32),
        ],
        scratch_shapes=[pltpu.VMEM((group, features, 2 * HD), BF16)],
        compiler_params=pltpu.CompilerParams(vmem_limit_bytes=VMEM_BYTES),
        cost_estimate=pl.CostEstimate(
            flops=8 * band * features * 2 * width,
            bytes_accessed=4 * features * width + 8 * rows * width,
            transcendentals=rows * band * heads,
        ),
        name="cross_attention",
    )(place, near, live, queries, grads, *own_pieces, *other_pieces)


def merge_kernel(group, own_ref, cross_ref, out_ref):
    for head in range(group):
        cols = slice(head * HD, (head + 1) * HD)
        out_ref[:, cols] = (own_ref[head].astype(F32) + cross_ref[:, cols]).astype(BF16)


def merged(own_tokens, cross_out):
    heads, rows, _ = own_tokens.shape
    group = 8
    flat = pl.BlockSpec((rows, group * HD), lambda i: (0, i))
    return pl.pallas_call(
        functools.partial(merge_kernel, group),
        grid=(heads // group,),
        in_specs=[pl.BlockSpec((group, rows, HD), lambda i: (i, 0, 0)), flat],
        out_specs=flat,
        out_shape=jax.ShapeDtypeStruct(cross_out.shape, BF16),
        compiler_params=pltpu.CompilerParams(vmem_limit_bytes=VMEM_BYTES),
        cost_estimate=pl.CostEstimate(
            flops=cross_out.size, bytes_accessed=8 * cross_out.size, transcendentals=0
        ),
        name="merge",
    )(own_tokens, cross_out)


def live_band(window_ids, live_counts, band_first, band_blocks, frame_rows):
    slots = jnp.arange(window_ids.shape[1], dtype=jnp.int32)
    blocks = band_first + jnp.arange(band_blocks, dtype=jnp.int32)
    hits = (window_ids[:, :, None] == blocks[None, None, :]) & (
        slots[None, :, None] < live_counts[:, None, None]
    )
    live = jnp.any(hits, axis=1).astype(F32)
    return jnp.repeat(jnp.repeat(live, AB, axis=1), frame_rows, axis=0)


def local(
    self_q,
    self_k,
    self_v,
    cross_q,
    audio,
    key_weight,
    value_weight,
    intersection,
    counts,
    cotangent,
):
    here = lax.axis_index("seq")
    layer = lax.axis_index("fsdp")
    layers = lax.axis_size("fsdp")
    rows = self_q.shape[1]
    members = lax.axis_size("seq")
    depth = key_weight.shape[0]

    even = (jnp.arange(members) % 2 == 0)[:, None, None]
    handed = jnp.where(even, key_weight[None], value_weight[None])
    start = lax.all_to_all(handed, "seq", split_axis=0, concat_axis=0, tiled=True)
    qkv = heads_first(self_q, self_k, self_v)
    start, qkv = lax.optimization_barrier((start, qkv))

    up, down = [start], [start]
    for _ in range((layers - 1) // 2):
        up.append(round_ring(up[-1], "fsdp", 1))
        down.append(round_ring(down[-1], "fsdp", -1))
    arrived = up[:-1] + down[1:-1]
    other_arrived = [from_other_core(piece) for piece in arrived]
    qkv = lax.all_to_all(qkv, "seq", split_axis=0, concat_axis=0, tiled=True)
    owned = audio.shape[1]
    half = owned // 2
    mine = audio[0]
    near = jnp.concatenate(
        [
            passed_along(mine[half:], "seq", 2),
            passed_along(mine, "seq", 1),
            mine,
            passed_along(mine, "seq", -1),
            passed_along(mine[:half], "seq", -2),
        ],
        axis=0,
    )
    qkv, other_arrived, near = lax.optimization_barrier((qkv, other_arrived, near))
    qkv = qkv.reshape(qkv.shape[0], 3, rows, HD)

    own_heads = attend_self(qkv, 0, 2)
    last_up, last_down, own_heads, qkv = lax.optimization_barrier(
        (up[-1], down[-1], own_heads, qkv)
    )
    middle = members // 2
    opposite = [
        round_ring(last_up[:middle], "fsdp", 1),
        round_ring(last_down[middle:], "fsdp", -1),
    ]
    last = [last_up, last_down]
    other_last = [from_other_core(piece) for piece in last]
    own_heads = attend_self(qkv, 1, 2, own_heads)
    opposite, other_last, own_heads = lax.optimization_barrier((opposite, other_last, own_heads))
    opposite = jnp.concatenate(opposite, axis=0)
    own_tokens = lax.all_to_all(
        own_heads.reshape(-1, rows, HD), "seq", split_axis=0, concat_axis=0, tiled=True
    )

    own_pieces = arrived + last + [opposite]
    other_pieces = other_arrived + other_last + [from_other_core(opposite)]
    steps = len(up)
    inner = steps - 1
    shifts = [-i for i in range(inner)] + [i for i in range(1, inner)] + [-inner, inner, steps]
    core = lax.rem(here, 2)
    place = jnp.concatenate(
        [
            lax.rem(layer + jnp.array([shift % layers for shift in shifts]), layers) * depth,
            jnp.stack([core * HD, (1 - core) * HD]),
        ]
    ).astype(jnp.int32)

    frames = intersection.shape[1]
    band_blocks = near.shape[0] // AB
    band_first = here * (owned // AB) - REACH
    live = live_band(intersection[0], counts[0], band_first, band_blocks, rows // frames)
    cross_out, band = cross_attention(
        place, near, live, cross_q[0], cotangent[0], own_pieces, other_pieces
    )
    block_out = merged(own_tokens, cross_out)

    total = band[half + owned : half + 2 * owned]
    band_b = band.astype(BF16)
    before = passed_along(band_b[half : half + owned], "seq", -1)
    after = passed_along(band_b[half + 2 * owned : half + 3 * owned], "seq", 1)
    far_before = passed_along(band_b[:half], "seq", -2)
    far_after = passed_along(band_b[half + 3 * owned :], "seq", 2)
    far = jnp.concatenate([far_after, far_before], axis=0)
    total = total + before.astype(F32) + after.astype(F32) + far.astype(F32)
    return (block_out[None], total[None])


def solution(mesh):
    in_specs = (
        P("fsdp", "seq", None),
        P("fsdp", "seq", None),
        P("fsdp", "seq", None),
        P("fsdp", "seq", None),
        P("fsdp", "seq", None),
        P("fsdp", "seq"),
        P("fsdp", "seq"),
        P("fsdp", "seq", None),
        P("fsdp", "seq"),
        P("fsdp", "seq", None),
    )
    out_specs = (P("fsdp", "seq", None), P("fsdp", "seq", None))
    return jax.shard_map(local, mesh=mesh, in_specs=in_specs, out_specs=out_specs, check_vma=False)
```

```python
import functools

import jax
import jax.numpy as jnp
from jax import lax
from jax.experimental import pallas as pl
from jax.experimental.pallas import tpu as pltpu
from jax.sharding import PartitionSpec as P

HD = 128
AB = 16
MAXB = 4
REACH = 3
SCALING = HD ** (-0.5)
EXP2_SCALING = SCALING * 1.4426950408889634
F32 = jnp.float32
BF16 = jnp.bfloat16
VMEM_BYTES = 60 * 1024 * 1024
CROSS_GROUP = 8


def passed_along(block, axis, distance):
    devices = range(lax.axis_size(axis))
    route = [(i - distance, i) for i in devices if i - distance in devices]
    return lax.ppermute(block, axis, route)


def round_ring(block, distance, core=None):
    layers = lax.axis_size("fsdp")
    members = range(lax.axis_size("seq"))
    route = [
        (i * layers + z, i * layers + (z + distance) % layers)
        for i in members
        for z in range(layers)
        if core is None or i % 2 == core
    ]
    return lax.ppermute(block, ("seq", "fsdp"), route)


def from_other_core(block, core=None):
    members = range(lax.axis_size("seq"))
    route = [(i, i ^ 1) for i in members if core is None or i % 2 == core]
    return lax.ppermute(block, "seq", route)


def heads_first_kernel(group, q_ref, k_ref, v_ref, out_ref):
    rows = q_ref.shape[0]
    for head in range(group):
        cols = slice(head * HD, (head + 1) * HD)
        out_ref[head, 0:rows] = q_ref[:, cols]
        out_ref[head, rows : 2 * rows] = k_ref[:, cols]
        out_ref[head, 2 * rows : 3 * rows] = v_ref[:, cols]


def heads_first(q_local, k_local, v_local):
    _, rows, width = q_local.shape
    heads = width // HD
    group = 8
    block = pl.BlockSpec((None, rows, group * HD), lambda i: (0, 0, i))
    return pl.pallas_call(
        functools.partial(heads_first_kernel, group),
        grid=(heads // group,),
        in_specs=[block] * 3,
        out_specs=pl.BlockSpec((group, 3 * rows, HD), lambda i: (i, 0, 0)),
        out_shape=jax.ShapeDtypeStruct((heads, 3 * rows, HD), BF16),
        compiler_params=pltpu.CompilerParams(vmem_limit_bytes=VMEM_BYTES),
        cost_estimate=pl.CostEstimate(
            flops=0, bytes_accessed=6 * rows * width * 2, transcendentals=0
        ),
        name="heads_first",
    )(q_local, k_local, v_local)


def self_attention_kernel(block_rows, block_keys, operands, *refs):
    q_ref, k_ref, v_ref = refs[:3]
    out_ref, keys_t, values_x, scores, tops = refs[operands:]
    chunk = q_ref.shape[1]
    length = k_ref.shape[0] * chunk
    key_blocks = length // block_keys
    query_blocks = out_ref.shape[0] // block_rows
    for piece in range(length // chunk):
        keys_t[:, piece * chunk : (piece + 1) * chunk] = k_ref[piece].T
        values_x[piece * chunk : (piece + 1) * chunk, :HD] = v_ref[piece]
    values_x[:, HD:] = jnp.ones((length, HD), BF16)
    per_block = block_rows // chunk

    def queries_of(block):
        rows = q_ref[pl.ds(block * per_block, per_block)]
        return rows.reshape(block_rows, HD)

    def highest(top, part):
        for group in range(part.shape[1] // HD):
            lanes = part[:, group * HD : (group + 1) * HD]
            top = lanes if top is None else jnp.maximum(top, lanes)
        return top

    def row_max(top):
        return jnp.broadcast_to(jnp.max(top, axis=1, keepdims=True), (block_rows, HD))

    first = queries_of(0)
    top = None
    for j in range(key_blocks):
        keys = slice(j * block_keys, (j + 1) * block_keys)
        part = jnp.dot(first, keys_t[:, keys], preferred_element_type=F32)
        scores[0, :, keys] = part
        top = highest(top, part)
    tops[0] = row_max(top)

    def body(i, carry):
        slot = lax.rem(i, 2)
        later = 1 - slot
        queries = queries_of(jnp.minimum(i + 1, query_blocks - 1))
        top_here = tops[slot][:, :1]
        top = None
        total = None
        for j in range(key_blocks):
            keys = slice(j * block_keys, (j + 1) * block_keys)
            part = jnp.dot(queries, keys_t[:, keys], preferred_element_type=F32)
            scores[later, :, keys] = part
            top = highest(top, part)
            raised = jnp.exp2((scores[slot, :, keys] - top_here) * EXP2_SCALING).astype(BF16)
            mixed = jnp.dot(raised, values_x[keys, :], preferred_element_type=F32)
            total = mixed if total is None else total + mixed
        tops[later] = row_max(top)
        rows = pl.ds(pl.multiple_of(i * block_rows, block_rows), block_rows)
        out_ref[rows, :] = (total[:, :HD] / total[:, HD:]).astype(BF16)
        return carry

    lax.fori_loop(0, query_blocks, body, 0)


def attend_self(qkv, part, parts, so_far=None):
    sources, _, rows, _ = qkv.shape
    length = sources * rows
    block_rows, block_keys = 512, 512
    q_sources = sources // parts

    def whole(which):
        return pl.BlockSpec((sources, None, rows, HD), lambda i: (0, which, 0, 0))

    operands = [qkv, qkv, qkv]
    in_specs = [
        pl.BlockSpec((q_sources, None, rows, HD), lambda i: (part, 0, 0, 0)),
        whole(1),
        whole(2),
    ]
    aliases = {}
    if so_far is not None:
        operands.append(so_far)
        in_specs.append(pl.BlockSpec(memory_space=pl.ANY))
        aliases = {3: 0}
    return pl.pallas_call(
        functools.partial(self_attention_kernel, block_rows, block_keys, len(operands)),
        grid=(1,),
        in_specs=in_specs,
        out_specs=pl.BlockSpec((length // parts, HD), lambda i: (part, 0)),
        out_shape=jax.ShapeDtypeStruct((length, HD), BF16),
        scratch_shapes=[
            pltpu.VMEM((HD, length), BF16),
            pltpu.VMEM((length, 2 * HD), BF16),
            pltpu.VMEM((2, block_rows, length), F32),
            pltpu.VMEM((2, block_rows, HD), F32),
        ],
        input_output_aliases=aliases,
        compiler_params=pltpu.CompilerParams(vmem_limit_bytes=VMEM_BYTES),
        cost_estimate=pl.CostEstimate(
            flops=8 * length * length * HD // parts,
            bytes_accessed=8 * length * HD,
            transcendentals=length * length // parts,
        ),
        name="self_attention",
    )(*operands)


def contract(a, b, dim_a, dim_b):
    return lax.dot_general(a, b, (((dim_a,), (dim_b,)), ((), ())), preferred_element_type=F32)


def cross_kernel(
    group,
    common,
    place_ref,
    near_ref,
    live_ref,
    q_ref,
    grad_ref,
    *refs,
):
    piece_refs = refs[: 2 * common]
    opposite_refs = refs[2 * common : 2 * common + 4]
    out_ref, audio_grad_ref, proj = refs[2 * common + 4 :]

    @pl.when(pl.program_id(0) == 0)
    def _():
        audio_grad_ref[...] = jnp.zeros_like(audio_grad_ref)

    depth = piece_refs[0].shape[1]

    def put(piece, kind, ref):
        lanes = pl.ds(pl.multiple_of(place_ref[common + 1 + kind], HD), HD)
        rows = pl.ds(pl.multiple_of(place_ref[piece], 32), depth)
        proj[:, rows, lanes] = ref[...]

    for kind in range(2):
        for piece in range(common):
            put(piece, kind, piece_refs[kind * common + piece])
    for core in range(2):

        @pl.when(place_ref[common + 3] == core)
        def _(core=core):
            put(common, 0, opposite_refs[core])
            put(common, 1, opposite_refs[2 + 1 - core])

    near = near_ref[...]
    live = live_ref[...] > 0
    heads = range(group)
    cols = [slice(head * HD, (head + 1) * HD) for head in heads]
    both = [
        jnp.dot(near, proj[head], preferred_element_type=F32).astype(BF16) for head in heads
    ]
    keys = [part[:, :HD] for part in both]
    values = [part[:, HD:] for part in both]
    scores = [contract(q_ref[:, cols[head]], keys[head], 1, 1) for head in heads]
    d_probs = [contract(grad_ref[:, cols[head]], values[head], 1, 1) for head in heads]
    weights = []
    for head in heads:
        masked = jnp.where(live, scores[head], -1e30)
        top = jnp.max(masked, axis=1, keepdims=True)
        raised = jnp.exp2((masked - top) * EXP2_SCALING)
        weights.append(raised / jnp.sum(raised, axis=1, keepdims=True))
    weights_b = [part.astype(BF16) for part in weights]
    d_scores = []
    for head in heads:
        weighed = weights[head] * d_probs[head]
        inner = jnp.sum(weighed, axis=1, keepdims=True)
        d_scores.append((weighed - weights[head] * inner).astype(BF16))
    for head in heads:
        out_ref[:, cols[head]] = jnp.dot(
            weights_b[head], values[head], preferred_element_type=F32
        )
    d_values = [
        contract(weights_b[head], grad_ref[:, cols[head]], 0, 0).astype(BF16) for head in heads
    ]
    d_keys = [
        (contract(d_scores[head], q_ref[:, cols[head]], 0, 0) * SCALING).astype(BF16)
        for head in heads
    ]
    sent = None
    for head in heads:
        d_both = jnp.concatenate([d_keys[head], d_values[head]], axis=1)
        term = contract(d_both, proj[head], 1, 1)
        sent = term if sent is None else sent + term
    audio_grad_ref[...] += sent


def cross_attention(place, near, live, queries, grads, pieces, opposite):
    heads, depth, _ = pieces[0].shape
    common = len(pieces) // 2
    features = depth * (common + 1)
    rows, width = queries.shape
    band = near.shape[0]
    group = CROSS_GROUP
    piece = pl.BlockSpec((group, depth, HD), lambda i: (i, 0, 0))
    return pl.pallas_call(
        functools.partial(cross_kernel, group, common),
        grid=(heads // group,),
        in_specs=[
            pl.BlockSpec(memory_space=pltpu.SMEM),
            pl.BlockSpec((band, features), lambda i: (0, 0)),
            pl.BlockSpec((rows, band), lambda i: (0, 0)),
            pl.BlockSpec((rows, group * HD), lambda i: (0, i)),
            pl.BlockSpec((rows, group * HD), lambda i: (0, i)),
        ]
        + [piece] * (2 * common + 4),
        out_specs=[
            pl.BlockSpec((rows, group * HD), lambda i: (0, i)),
            pl.BlockSpec((band, features), lambda i: (0, 0)),
        ],
        out_shape=[
            jax.ShapeDtypeStruct((rows, width), F32),
            jax.ShapeDtypeStruct((band, features), F32),
        ],
        scratch_shapes=[pltpu.VMEM((group, features, 2 * HD), BF16)],
        compiler_params=pltpu.CompilerParams(vmem_limit_bytes=VMEM_BYTES),
        cost_estimate=pl.CostEstimate(
            flops=8 * band * features * 2 * width,
            bytes_accessed=4 * features * width + 8 * rows * width,
            transcendentals=rows * band * heads,
        ),
        name="cross_attention",
    )(place, near, live, queries, grads, *pieces, *opposite)


def merge_kernel(group, own_ref, cross_ref, out_ref):
    for head in range(group):
        cols = slice(head * HD, (head + 1) * HD)
        out_ref[:, cols] = (own_ref[head].astype(F32) + cross_ref[:, cols]).astype(BF16)


def merged(own_tokens, cross_out):
    heads, rows, _ = own_tokens.shape
    group = 8
    flat = pl.BlockSpec((rows, group * HD), lambda i: (0, i))
    return pl.pallas_call(
        functools.partial(merge_kernel, group),
        grid=(heads // group,),
        in_specs=[pl.BlockSpec((group, rows, HD), lambda i: (i, 0, 0)), flat],
        out_specs=flat,
        out_shape=jax.ShapeDtypeStruct(cross_out.shape, BF16),
        compiler_params=pltpu.CompilerParams(vmem_limit_bytes=VMEM_BYTES),
        cost_estimate=pl.CostEstimate(
            flops=cross_out.size, bytes_accessed=8 * cross_out.size, transcendentals=0
        ),
        name="merge",
    )(own_tokens, cross_out)


def live_band(window_ids, live_counts, band_first, band_blocks, frame_rows):
    slots = jnp.arange(window_ids.shape[1], dtype=jnp.int32)
    blocks = band_first + jnp.arange(band_blocks, dtype=jnp.int32)
    hits = (window_ids[:, :, None] == blocks[None, None, :]) & (
        slots[None, :, None] < live_counts[:, None, None]
    )
    live = jnp.any(hits, axis=1).astype(F32)
    return jnp.repeat(jnp.repeat(live, AB, axis=1), frame_rows, axis=0)


def local(
    self_q,
    self_k,
    self_v,
    cross_q,
    audio,
    key_weight,
    value_weight,
    intersection,
    counts,
    cotangent,
):
    here = lax.axis_index("seq")
    layer = lax.axis_index("fsdp")
    layers = lax.axis_size("fsdp")
    members = lax.axis_size("seq")
    core = lax.rem(here, 2)
    rows = self_q.shape[1]
    depth = key_weight.shape[0]
    owned = audio.shape[1]
    half = owned // 2

    even = (jnp.arange(members) % 2 == 0)[:, None, None]
    handed = jnp.where(even, key_weight[None], value_weight[None])
    start = lax.all_to_all(handed, "seq", split_axis=0, concat_axis=0, tiled=True)

    qkv = heads_first(self_q, self_k, self_v)
    mine = audio[0]
    near = jnp.concatenate(
        [
            passed_along(mine[half:], "seq", 2),
            passed_along(mine, "seq", 1),
            mine,
            passed_along(mine, "seq", -1),
            passed_along(mine[:half], "seq", -2),
        ],
        axis=0,
    )
    frames = intersection.shape[1]
    band_blocks = near.shape[0] // AB
    band_first = here * (owned // AB) - REACH
    live = live_band(intersection[0], counts[0], band_first, band_blocks, rows // frames)
    steps = (layers - 1) // 2
    shifts = [-i for i in range(steps)] + [i for i in range(1, steps)]
    shifts += [-steps, steps, layers // 2]
    place = jnp.concatenate(
        [
            lax.rem(layer + jnp.array([shift % layers for shift in shifts]), layers) * depth,
            jnp.stack([core * HD, (1 - core) * HD, core]),
        ]
    ).astype(jnp.int32)
    start, qkv, near, live, place = lax.optimization_barrier((start, qkv, near, live, place))

    up, down = [start], [start]
    for _ in range(steps):
        up.append(round_ring(up[-1], 1))
        down.append(round_ring(down[-1], -1))
    arrived = up[:-1] + down[1:-1]
    other_arrived = [from_other_core(piece) for piece in arrived]
    qkv = lax.all_to_all(qkv, "seq", split_axis=0, concat_axis=0, tiled=True)
    qkv, other_arrived = lax.optimization_barrier((qkv, other_arrived))
    qkv = qkv.reshape(qkv.shape[0], 3, rows, HD)

    own_heads = attend_self(qkv, 0, 2)
    last_up, last_down, own_heads, qkv = lax.optimization_barrier(
        (up[-1], down[-1], own_heads, qkv)
    )
    opposite = [round_ring(last_up, 1, 0), round_ring(last_down, -1, 1)]
    last = [last_up, last_down]
    other_last = [from_other_core(piece) for piece in last]
    own_heads = attend_self(qkv, 1, 2, own_heads)
    opposite, other_last, own_heads = lax.optimization_barrier((opposite, other_last, own_heads))
    own_tokens = lax.all_to_all(
        own_heads.reshape(-1, rows, HD), "seq", split_axis=0, concat_axis=0, tiled=True
    )
    other_opposite = [from_other_core(opposite[0], 0), from_other_core(opposite[1], 1)]

    cross_out, band = cross_attention(
        place,
        near,
        live,
        cross_q[0],
        cotangent[0],
        arrived + last + other_arrived + other_last,
        opposite + other_opposite,
    )
    block_out = merged(own_tokens, cross_out)

    total = band[half + owned : half + 2 * owned]
    band_b = band.astype(BF16)
    before = passed_along(band_b[half : half + owned], "seq", -1)
    after = passed_along(band_b[half + 2 * owned : half + 3 * owned], "seq", 1)
    far_before = passed_along(band_b[:half], "seq", -2)
    far_after = passed_along(band_b[half + 3 * owned :], "seq", 2)
    far = jnp.concatenate([far_after, far_before], axis=0)
    total = total + before.astype(F32) + after.astype(F32) + far.astype(F32)
    return (block_out[None], total[None])


def solution(mesh):
    in_specs = (
        P("fsdp", "seq", None),
        P("fsdp", "seq", None),
        P("fsdp", "seq", None),
        P("fsdp", "seq", None),
        P("fsdp", "seq", None),
        P("fsdp", "seq"),
        P("fsdp", "seq"),
        P("fsdp", "seq", None),
        P("fsdp", "seq"),
        P("fsdp", "seq", None),
    )
    out_specs = (P("fsdp", "seq", None), P("fsdp", "seq", None))
    return jax.shard_map(local, mesh=mesh, in_specs=in_specs, out_specs=out_specs, check_vma=False)
```

```python
import functools

import jax
import jax.numpy as jnp
from jax import lax
from jax.experimental import pallas as pl
from jax.experimental.pallas import tpu as pltpu
from jax.sharding import PartitionSpec as P

HD = 128
AB = 16
REACH = 3
PAD = 16
SCALING = HD ** (-0.5)
EXP2_SCALING = SCALING * 1.4426950408889634
F32 = jnp.float32
BF16 = jnp.bfloat16
VMEM_BYTES = 48 * 1024 * 1024


def kernel_params():
    return pltpu.CompilerParams(vmem_limit_bytes=VMEM_BYTES)


def handed_over(parts):
    return lax.all_to_all(parts, "seq", split_axis=0, concat_axis=0, tiled=True)


def gathered_by_doubling(block, axis):
    size = lax.axis_size(axis)
    here = lax.axis_index(axis)
    step = 1
    while step < size:
        other = lax.ppermute(block, axis, [(i, i ^ step) for i in range(size)])
        upper = (here & step) != 0
        block = jnp.concatenate(
            [jnp.where(upper, other, block), jnp.where(upper, block, other)], axis=0
        )
        step *= 2
    return block


def from_other_core(block):
    size = lax.axis_size("seq")
    return lax.ppermute(block, "seq", [(i, i ^ 1) for i in range(size)])


def contract(a, b, dim_a, dim_b):
    return lax.dot_general(a, b, (((dim_a,), (dim_b,)), ((), ())), preferred_element_type=F32)


def self_heads_kernel(group, q_ref, k_ref, v_ref, out_ref):
    rows = q_ref.shape[0]
    for head in range(group):
        cols = slice(head * HD, (head + 1) * HD)
        out_ref[head, 0:rows] = q_ref[:, cols]
        out_ref[head, rows : 2 * rows] = k_ref[:, cols]
        out_ref[head, 2 * rows : 3 * rows] = v_ref[:, cols]


def self_heads(q_local, k_local, v_local):
    _, rows, width = q_local.shape
    heads = width // HD
    group = 8
    block = pl.BlockSpec((None, rows, group * HD), lambda i: (0, 0, i))
    return pl.pallas_call(
        functools.partial(self_heads_kernel, group),
        grid=(heads // group,),
        in_specs=[block] * 3,
        out_specs=pl.BlockSpec((group, 3 * rows, HD), lambda i: (i, 0, 0)),
        out_shape=jax.ShapeDtypeStruct((heads, 3 * rows, HD), BF16),
        compiler_params=kernel_params(),
        cost_estimate=pl.CostEstimate(
            flops=0, bytes_accessed=6 * rows * width * 2, transcendentals=0
        ),
        name="self_heads",
    )(q_local, k_local, v_local)


def cross_heads_kernel(group, q_ref, grad_ref, audio_ref, live_ref, out_ref):
    rows = q_ref.shape[0]
    owned, features = audio_ref.shape
    chunks = features // HD // 2
    for head in range(group):
        cols = slice(head * HD, (head + 1) * HD)
        out_ref[head, 0:rows] = q_ref[:, cols]
        out_ref[head, rows : 2 * rows] = grad_ref[:, cols]
        for chunk in range(chunks):
            first = 2 * rows + chunk * owned
            lane = (head % 2 * chunks + chunk) * HD
            out_ref[head, first : first + owned] = audio_ref[:, lane : lane + HD]
        out_ref[head, 2 * rows + chunks * owned :] = live_ref[...]


def cross_heads(queries, grads, audio, live):
    _, rows, width = queries.shape
    _, owned, features = audio.shape
    heads = width // HD
    group = 8
    total = 2 * rows + owned * (features // HD // 2) + PAD
    block = pl.BlockSpec((None, rows, group * HD), lambda i: (0, 0, i))
    return pl.pallas_call(
        functools.partial(cross_heads_kernel, group),
        grid=(heads // group,),
        in_specs=[
            block,
            block,
            pl.BlockSpec((None, owned, features), lambda i: (0, 0, 0)),
            pl.BlockSpec((PAD, HD), lambda i: (0, 0)),
        ],
        out_specs=pl.BlockSpec((group, total, HD), lambda i: (i, 0, 0)),
        out_shape=jax.ShapeDtypeStruct((heads, total, HD), BF16),
        compiler_params=kernel_params(),
        cost_estimate=pl.CostEstimate(
            flops=0, bytes_accessed=5 * rows * width * 2, transcendentals=0
        ),
        name="cross_heads",
    )(queries, grads, audio, live)


def cross_kernel(
    rows,
    place_ref,
    got_ref,
    other_ref,
    proj_ref,
    out_ref,
    sent_ref,
    audio,
    keys,
    values,
    d_keys,
    d_values,
):
    sources = got_ref.shape[0]
    owned = AB * 2
    chunks = other_ref.shape[1] // owned
    length = sources * owned
    edge = REACH * AB
    band = HD
    at_once = 8
    first_audio = 2 * rows

    for chunk in range(chunks):
        own_lanes = pl.ds(pl.multiple_of(place_ref[0] + chunk * HD, HD), HD)
        other_lanes = pl.ds(pl.multiple_of(place_ref[1] + chunk * HD, HD), HD)
        own_rows = slice(first_audio + chunk * owned, first_audio + (chunk + 1) * owned)
        other_rows = slice(chunk * owned, (chunk + 1) * owned)
        audio[:, own_lanes] = got_ref[:, own_rows].reshape(length, HD)
        audio[:, other_lanes] = other_ref[:, other_rows].reshape(length, HD)

    keys[...] = jnp.zeros_like(keys)
    values[...] = jnp.zeros_like(values)
    d_keys[...] = jnp.zeros_like(d_keys)
    d_values[...] = jnp.zeros_like(d_values)
    step = 256
    for i in range(length // step):
        both = jnp.dot(
            audio[i * step : (i + 1) * step], proj_ref[...], preferred_element_type=F32
        ).astype(BF16)
        keys[edge + i * step : edge + (i + 1) * step] = both[:, :HD]
        values[edge + i * step : edge + (i + 1) * step] = both[:, HD:]

    def some(block, carry):
        sources_here = [block * at_once + i for i in range(at_once)]
        bands = [pl.ds(pl.multiple_of(t * owned, owned), band) for t in sources_here]
        k = [keys[b] for b in bands]
        v = [values[b] for b in bands]
        scores = [contract(got_ref[t, 0:rows], k[i], 1, 1) for i, t in enumerate(sources_here)]
        d_probs = [
            contract(got_ref[t, rows : 2 * rows], v[i], 1, 1)
            for i, t in enumerate(sources_here)
        ]
        weights = []
        for i, t in enumerate(sources_here):
            masks = got_ref[t, first_audio + chunks * owned :].astype(F32)
            live = jnp.concatenate(
                [jnp.broadcast_to(masks[f : f + 1], (rows // 2, band)) for f in range(2)], axis=0
            )
            masked = jnp.where(live > 0, scores[i], -1e30)
            top = jnp.max(masked, axis=1, keepdims=True)
            raised = jnp.exp2((masked - top) * EXP2_SCALING)
            weights.append(raised / jnp.sum(raised, axis=1, keepdims=True))
        weights_b = [part.astype(BF16) for part in weights]
        d_scores = []
        for i in range(at_once):
            weighed = weights[i] * d_probs[i]
            inner = jnp.sum(weighed, axis=1, keepdims=True)
            d_scores.append((weighed - weights[i] * inner).astype(BF16))
        for i, t in enumerate(sources_here):
            out_ref[t] = jnp.dot(weights_b[i], v[i], preferred_element_type=F32)
        for i, t in enumerate(sources_here):
            d_values[bands[i]] += contract(weights_b[i], got_ref[t, rows : 2 * rows], 0, 0)
            d_keys[bands[i]] += contract(d_scores[i], got_ref[t, 0:rows], 0, 0)
        return carry

    lax.fori_loop(0, sources // at_once, some, 0)

    for i in range(length // step):
        here = slice(edge + i * step, edge + (i + 1) * step)
        d_both = jnp.concatenate(
            [(d_keys[here] * SCALING).astype(BF16), d_values[here].astype(BF16)], axis=1
        )
        term = contract(d_both, proj_ref[...], 1, 1).astype(BF16)
        per = step // owned
        for chunk in range(2 * chunks):
            sent_ref[i * per : (i + 1) * per, chunk * owned : (chunk + 1) * owned] = term[
                :, chunk * HD : (chunk + 1) * HD
            ].reshape(per, owned, HD)


def cross_attention(place, got, other_audio, proj, rows):
    sources, total, _ = got.shape
    audio_rows = other_audio.shape[1]
    features = proj.shape[0]
    owned = 2 * AB
    length = sources * owned
    padded = length + HD - owned
    return pl.pallas_call(
        functools.partial(cross_kernel, rows),
        grid=(1,),
        in_specs=[
            pl.BlockSpec(memory_space=pltpu.SMEM),
            pl.BlockSpec((sources, total, HD), lambda i: (0, 0, 0)),
            pl.BlockSpec((sources, audio_rows, HD), lambda i: (0, 0, 0)),
            pl.BlockSpec((features, 2 * HD), lambda i: (0, 0)),
        ],
        out_specs=[
            pl.BlockSpec((sources, rows, HD), lambda i: (0, 0, 0)),
            pl.BlockSpec((sources, 2 * audio_rows, HD), lambda i: (0, 0, 0)),
        ],
        out_shape=[
            jax.ShapeDtypeStruct((sources, rows, HD), F32),
            jax.ShapeDtypeStruct((sources, 2 * audio_rows, HD), BF16),
        ],
        scratch_shapes=[
            pltpu.VMEM((length, features), BF16),
            pltpu.VMEM((padded, HD), BF16),
            pltpu.VMEM((padded, HD), BF16),
            pltpu.VMEM((padded, HD), F32),
            pltpu.VMEM((padded, HD), F32),
        ],
        compiler_params=kernel_params(),
        cost_estimate=pl.CostEstimate(
            flops=8 * length * features * HD + 10 * sources * rows * HD * HD,
            bytes_accessed=2 * (got.size + 3 * other_audio.size + proj.size),
            transcendentals=sources * rows * HD,
        ),
        name="cross_attention",
    )(place, got, other_audio, proj)


def self_attention_kernel(
    block_rows,
    block_keys,
    q_ref,
    k_ref,
    v_ref,
    cross_ref,
    out_ref,
    keys_t,
    values_x,
    scores,
    tops,
):
    chunk = q_ref.shape[1]
    length = k_ref.shape[0] * chunk
    key_blocks = length // block_keys
    query_blocks = length // block_rows
    for piece in range(length // chunk):
        keys_t[:, piece * chunk : (piece + 1) * chunk] = k_ref[piece].T
        values_x[piece * chunk : (piece + 1) * chunk, :HD] = v_ref[piece]
    values_x[:, HD:] = jnp.ones((length, HD), BF16)
    per_block = block_rows // chunk

    def queries_of(block):
        rows = q_ref[pl.ds(block * per_block, per_block)]
        return rows.reshape(block_rows, HD)

    def highest(top, part):
        for group in range(part.shape[1] // HD):
            lanes = part[:, group * HD : (group + 1) * HD]
            top = lanes if top is None else jnp.maximum(top, lanes)
        return top

    def row_max(top):
        return jnp.broadcast_to(jnp.max(top, axis=1, keepdims=True), (block_rows, HD))

    first = queries_of(0)
    top = None
    for j in range(key_blocks):
        keys = slice(j * block_keys, (j + 1) * block_keys)
        part = jnp.dot(first, keys_t[:, keys], preferred_element_type=F32)
        scores[0, :, keys] = part
        top = highest(top, part)
    tops[0] = row_max(top)

    def body(i, carry):
        slot = lax.rem(i, 2)
        later = 1 - slot
        queries = queries_of(jnp.minimum(i + 1, query_blocks - 1))
        top_here = tops[slot][:, :1]
        top = None
        total = None
        for j in range(key_blocks):
            keys = slice(j * block_keys, (j + 1) * block_keys)
            part = jnp.dot(queries, keys_t[:, keys], preferred_element_type=F32)
            scores[later, :, keys] = part
            top = highest(top, part)
            raised = jnp.exp2((scores[slot, :, keys] - top_here) * EXP2_SCALING).astype(BF16)
            mixed = jnp.dot(raised, values_x[keys, :], preferred_element_type=F32)
            total = mixed if total is None else total + mixed
        tops[later] = row_max(top)
        own = (total[:, :HD] / total[:, HD:]).astype(BF16).astype(F32)
        rows = pl.ds(i * per_block, per_block)
        own = own.reshape(per_block, chunk, HD)
        out_ref[rows] = (own + cross_ref[rows]).astype(BF16)
        return carry

    lax.fori_loop(0, query_blocks, body, 0)


def attend_self(qkv, cross_out):
    sources, _, rows, _ = qkv.shape
    length = sources * rows
    block_rows, block_keys = 512, 512

    def whole(which):
        return pl.BlockSpec((sources, None, rows, HD), lambda i: (0, which, 0, 0))

    flat = pl.BlockSpec((sources, rows, HD), lambda i: (0, 0, 0))
    return pl.pallas_call(
        functools.partial(self_attention_kernel, block_rows, block_keys),
        grid=(1,),
        in_specs=[whole(0), whole(1), whole(2), flat],
        out_specs=flat,
        out_shape=jax.ShapeDtypeStruct((sources, rows, HD), BF16),
        scratch_shapes=[
            pltpu.VMEM((HD, length), BF16),
            pltpu.VMEM((length, 2 * HD), BF16),
            pltpu.VMEM((2, block_rows, length), F32),
            pltpu.VMEM((2, block_rows, HD), F32),
        ],
        compiler_params=kernel_params(),
        cost_estimate=pl.CostEstimate(
            flops=8 * length * length * HD,
            bytes_accessed=12 * length * HD,
            transcendentals=length * length,
        ),
        name="self_attention",
    )(qkv, qkv, qkv, cross_out)


def tokens_kernel(group, own_ref, out_ref):
    for head in range(group):
        out_ref[:, head * HD : (head + 1) * HD] = own_ref[head]


def heads_beside(own_tokens):
    heads, rows, _ = own_tokens.shape
    group = 8
    return pl.pallas_call(
        functools.partial(tokens_kernel, group),
        grid=(heads // group,),
        in_specs=[pl.BlockSpec((group, rows, HD), lambda i: (i, 0, 0))],
        out_specs=pl.BlockSpec((None, rows, group * HD), lambda i: (0, 0, i)),
        out_shape=jax.ShapeDtypeStruct((1, rows, heads * HD), BF16),
        compiler_params=kernel_params(),
        cost_estimate=pl.CostEstimate(
            flops=0, bytes_accessed=4 * rows * heads * HD, transcendentals=0
        ),
        name="heads_beside",
    )(own_tokens)


def sum_kernel(terms_ref, out_ref):
    owned = out_ref.shape[0]
    total = jnp.sum(terms_ref[...].astype(F32), axis=0)
    for chunk in range(total.shape[0] // owned):
        out_ref[:, chunk * HD : (chunk + 1) * HD] = total[chunk * owned : (chunk + 1) * owned]


def summed(terms, owned):
    heads, total, _ = terms.shape
    features = total // owned * HD
    return pl.pallas_call(
        sum_kernel,
        grid=(1,),
        in_specs=[pl.BlockSpec((heads, total, HD), lambda i: (0, 0, 0))],
        out_specs=pl.BlockSpec((None, owned, features), lambda i: (0, 0, 0)),
        out_shape=jax.ShapeDtypeStruct((1, owned, features), F32),
        compiler_params=kernel_params(),
        cost_estimate=pl.CostEstimate(
            flops=terms.size, bytes_accessed=2 * terms.size, transcendentals=0
        ),
        name="summed",
    )(terms)


def live_band(window_ids, live_counts, band_first, band_blocks):
    slots = jnp.arange(window_ids.shape[1], dtype=jnp.int32)
    blocks = band_first + jnp.arange(band_blocks, dtype=jnp.int32)
    hits = (window_ids[:, :, None] == blocks[None, None, :]) & (
        slots[None, :, None] < live_counts[:, None, None]
    )
    live = jnp.any(hits, axis=1).astype(BF16)
    live = jnp.repeat(live, AB, axis=1)
    return jnp.pad(live, ((0, PAD - live.shape[0]), (0, 0)))


def local(
    self_q,
    self_k,
    self_v,
    cross_q,
    audio,
    key_weight,
    value_weight,
    intersection,
    counts,
    cotangent,
):
    here = lax.axis_index("seq")
    core = lax.rem(here, 2)
    rows = self_q.shape[1]
    owned, features = audio.shape[1:]

    live = live_band(intersection[0], counts[0], here * 2 - REACH, HD // AB)
    cross = cross_heads(cross_q, cotangent, audio, live)
    cross, key_weight, value_weight = lax.optimization_barrier((cross, key_weight, value_weight))
    cross = handed_over(cross)

    both = jnp.concatenate([key_weight, value_weight], axis=1)
    proj = gathered_by_doubling(both[None], "fsdp").reshape(-1, 2 * HD)
    place = jnp.stack([core, 1 - core]).astype(jnp.int32) * (features // 2)
    qkv = self_heads(self_q, self_k, self_v)
    cross, qkv, proj, place = lax.optimization_barrier((cross, qkv, proj, place))

    qkv = handed_over(qkv).reshape(-1, 3, rows, HD)
    other_audio = from_other_core(cross[:, 2 * rows : cross.shape[1] - PAD])
    cross_out, sent = cross_attention(place, cross, other_audio, proj, rows)
    terms = handed_over(sent)
    own_heads = attend_self(qkv, cross_out)
    own_heads, terms = lax.optimization_barrier((own_heads, terms))
    own_tokens = handed_over(own_heads)
    audio_grad = summed(terms, owned)
    return (heads_beside(own_tokens), audio_grad)


def solution(mesh):
    in_specs = (
        P("fsdp", "seq", None),
        P("fsdp", "seq", None),
        P("fsdp", "seq", None),
        P("fsdp", "seq", None),
        P("fsdp", "seq", None),
        P("fsdp", "seq"),
        P("fsdp", "seq"),
        P("fsdp", "seq", None),
        P("fsdp", "seq"),
        P("fsdp", "seq", None),
    )
    out_specs = (P("fsdp", "seq", None), P("fsdp", "seq", None))
    return jax.shard_map(local, mesh=mesh, in_specs=in_specs, out_specs=out_specs, check_vma=False)
```

```python
import functools

import jax
import jax.numpy as jnp
from jax import lax
from jax.experimental import pallas as pl
from jax.experimental.pallas import tpu as pltpu
from jax.sharding import PartitionSpec as P

HD = 128
AB = 16
REACH = 3
PAD = 16
SCALING = HD ** (-0.5)
EXP2_SCALING = SCALING * 1.4426950408889634
F32 = jnp.float32
BF16 = jnp.bfloat16
MIB = 1024 * 1024


def kernel_params(mib=48):
    return pltpu.CompilerParams(vmem_limit_bytes=mib * MIB)


def handed_over(parts):
    return lax.all_to_all(parts, "seq", split_axis=0, concat_axis=0, tiled=True)


def gathered_by_doubling(block, axis):
    size = lax.axis_size(axis)
    here = lax.axis_index(axis)
    step = 1
    while step < size:
        other = lax.ppermute(block, axis, [(i, i ^ step) for i in range(size)])
        upper = (here & step) != 0
        block = jnp.concatenate(
            [jnp.where(upper, other, block), jnp.where(upper, block, other)], axis=0
        )
        step *= 2
    return block


def from_other_core(block):
    size = lax.axis_size("seq")
    return lax.ppermute(block, "seq", [(i, i ^ 1) for i in range(size)])


def contract(a, b, dim_a, dim_b):
    return lax.dot_general(a, b, (((dim_a,), (dim_b,)), ((), ())), preferred_element_type=F32)


def self_heads_kernel(group, q_ref, k_ref, v_ref, audio_ref, out_ref):
    rows = q_ref.shape[0]
    owned, features = audio_ref.shape
    chunks = features // HD // 2
    for head in range(group):
        cols = slice(head * HD, (head + 1) * HD)
        out_ref[head, 0:rows] = q_ref[:, cols]
        out_ref[head, rows : 2 * rows] = k_ref[:, cols]
        out_ref[head, 2 * rows : 3 * rows] = v_ref[:, cols]
        for chunk in range(chunks):
            first = 3 * rows + chunk * owned
            lane = (head % 2 * chunks + chunk) * HD
            out_ref[head, first : first + owned] = audio_ref[:, lane : lane + HD]


def self_heads(q_local, k_local, v_local, audio):
    _, rows, width = q_local.shape
    _, owned, features = audio.shape
    heads = width // HD
    group = 4
    total = 3 * rows + owned * (features // HD // 2)
    block = pl.BlockSpec((None, rows, group * HD), lambda i: (0, 0, i))
    return pl.pallas_call(
        functools.partial(self_heads_kernel, group),
        grid=(heads // group,),
        in_specs=[block] * 3 + [pl.BlockSpec((None, owned, features), lambda i: (0, 0, 0))],
        out_specs=pl.BlockSpec((group, total, HD), lambda i: (i, 0, 0)),
        out_shape=jax.ShapeDtypeStruct((heads, total, HD), BF16),
        compiler_params=kernel_params(60),
        cost_estimate=pl.CostEstimate(
            flops=0, bytes_accessed=7 * rows * width * 2, transcendentals=0
        ),
        name="self_heads",
    )(q_local, k_local, v_local, audio)


def cross_heads_kernel(group, ids_ref, counts_ref, first_ref, q_ref, grad_ref, out_ref):
    rows = q_ref.shape[0]
    frames, slots = ids_ref.shape
    blocks = first_ref[0] + lax.broadcasted_iota(jnp.int32, (PAD, HD), 1) // AB
    row = lax.broadcasted_iota(jnp.int32, (PAD, HD), 0)
    live = jnp.zeros((PAD, HD), F32)
    for frame in range(frames):
        for slot in range(slots):
            hit = (blocks == ids_ref[frame, slot]) & (row == frame)
            hit = hit & (counts_ref[frame] > slot)
            live = jnp.where(hit, 1.0, live)
    live = live.astype(BF16)
    for head in range(group):
        cols = slice(head * HD, (head + 1) * HD)
        out_ref[head, 0:rows] = q_ref[:, cols]
        out_ref[head, rows : 2 * rows] = grad_ref[:, cols]
        out_ref[head, 2 * rows :] = live


def cross_heads(window_ids, live_counts, band_first, queries, grads):
    _, rows, width = queries.shape
    heads = width // HD
    group = 8
    total = 2 * rows + PAD
    block = pl.BlockSpec((None, rows, group * HD), lambda i: (0, 0, i))
    scalars = pl.BlockSpec(memory_space=pltpu.SMEM)
    return pl.pallas_call(
        functools.partial(cross_heads_kernel, group),
        grid=(heads // group,),
        in_specs=[scalars, scalars, scalars, block, block],
        out_specs=pl.BlockSpec((group, total, HD), lambda i: (i, 0, 0)),
        out_shape=jax.ShapeDtypeStruct((heads, total, HD), BF16),
        compiler_params=kernel_params(60),
        cost_estimate=pl.CostEstimate(
            flops=0, bytes_accessed=4 * rows * width * 2, transcendentals=0
        ),
        name="cross_heads",
    )(window_ids, live_counts, band_first, queries, grads)


def cross_kernel(
    rows,
    place_ref,
    got_ref,
    mine_ref,
    other_ref,
    proj_ref,
    own_ref,
    out_ref,
    audio,
    keys,
    values,
    d_keys,
    d_values,
):
    sources = got_ref.shape[0]
    owned = AB * 2
    chunks = other_ref.shape[1] // owned
    length = sources * owned
    edge = REACH * AB
    band = HD
    at_once = 8

    for chunk in range(chunks):
        own_lanes = pl.ds(pl.multiple_of(place_ref[0] + chunk * HD, HD), HD)
        other_lanes = pl.ds(pl.multiple_of(place_ref[1] + chunk * HD, HD), HD)
        chunk_rows = slice(chunk * owned, (chunk + 1) * owned)
        audio[:, own_lanes] = mine_ref[:, chunk_rows].reshape(length, HD)
        audio[:, other_lanes] = other_ref[:, chunk_rows].reshape(length, HD)

    keys[...] = jnp.zeros_like(keys)
    values[...] = jnp.zeros_like(values)
    d_keys[...] = jnp.zeros_like(d_keys)
    d_values[...] = jnp.zeros_like(d_values)
    step = 256
    for i in range(length // step):
        both = jnp.dot(
            audio[i * step : (i + 1) * step], proj_ref[...], preferred_element_type=F32
        ).astype(BF16)
        keys[edge + i * step : edge + (i + 1) * step] = both[:, :HD]
        values[edge + i * step : edge + (i + 1) * step] = both[:, HD:]

    def some(block, carry):
        sources_here = [block * at_once + i for i in range(at_once)]
        bands = [pl.ds(pl.multiple_of(t * owned, owned), band) for t in sources_here]
        k = [keys[b] for b in bands]
        v = [values[b] for b in bands]
        scores = [contract(got_ref[t, 0:rows], k[i], 1, 1) for i, t in enumerate(sources_here)]
        d_probs = [
            contract(got_ref[t, rows : 2 * rows], v[i], 1, 1)
            for i, t in enumerate(sources_here)
        ]
        weights = []
        for i, t in enumerate(sources_here):
            masks = got_ref[t, 2 * rows :].astype(F32)
            live = jnp.concatenate(
                [jnp.broadcast_to(masks[f : f + 1], (rows // 2, band)) for f in range(2)], axis=0
            )
            masked = jnp.where(live > 0, scores[i], -1e30)
            top = jnp.max(masked, axis=1, keepdims=True)
            raised = jnp.exp2((masked - top) * EXP2_SCALING)
            weights.append(raised / jnp.sum(raised, axis=1, keepdims=True))
        weights_b = [part.astype(BF16) for part in weights]
        d_scores = []
        for i in range(at_once):
            weighed = weights[i] * d_probs[i]
            inner = jnp.sum(weighed, axis=1, keepdims=True)
            d_scores.append((weighed - weights[i] * inner).astype(BF16))
        for i, t in enumerate(sources_here):
            mixed = jnp.dot(weights_b[i], v[i], preferred_element_type=F32)
            out_ref[t, 0:rows] = (own_ref[t].astype(F32) + mixed).astype(BF16)
        for i, t in enumerate(sources_here):
            d_values[bands[i]] += contract(weights_b[i], got_ref[t, rows : 2 * rows], 0, 0)
            d_keys[bands[i]] += contract(d_scores[i], got_ref[t, 0:rows], 0, 0)
        return carry

    lax.fori_loop(0, sources // at_once, some, 0)

    for i in range(length // step):
        here = slice(edge + i * step, edge + (i + 1) * step)
        d_both = jnp.concatenate(
            [(d_keys[here] * SCALING).astype(BF16), d_values[here].astype(BF16)], axis=1
        )
        term = contract(d_both, proj_ref[...], 1, 1).astype(BF16)
        per = step // owned
        for chunk in range(2 * chunks):
            first = rows + chunk * owned
            out_ref[i * per : (i + 1) * per, first : first + owned] = term[
                :, chunk * HD : (chunk + 1) * HD
            ].reshape(per, owned, HD)


def cross_attention(place, got, mine, other, proj, own_heads):
    sources, rows, _ = own_heads.shape
    total = got.shape[1]
    audio_rows = mine.shape[1]
    features = proj.shape[0]
    owned = 2 * AB
    length = sources * owned
    padded = length + HD - owned

    def whole(*shape):
        return pl.BlockSpec(shape, lambda i: (0,) * len(shape))

    return pl.pallas_call(
        functools.partial(cross_kernel, rows),
        grid=(1,),
        in_specs=[
            pl.BlockSpec(memory_space=pltpu.SMEM),
            whole(sources, total, HD),
            whole(sources, audio_rows, HD),
            whole(sources, audio_rows, HD),
            whole(features, 2 * HD),
            whole(sources, rows, HD),
        ],
        out_specs=whole(sources, rows + 2 * audio_rows, HD),
        out_shape=jax.ShapeDtypeStruct((sources, rows + 2 * audio_rows, HD), BF16),
        scratch_shapes=[
            pltpu.VMEM((length, features), BF16),
            pltpu.VMEM((padded, HD), BF16),
            pltpu.VMEM((padded, HD), BF16),
            pltpu.VMEM((padded, HD), F32),
            pltpu.VMEM((padded, HD), F32),
        ],
        compiler_params=kernel_params(),
        cost_estimate=pl.CostEstimate(
            flops=8 * length * features * HD + 10 * sources * rows * HD * HD,
            bytes_accessed=2 * (got.size + 4 * mine.size + proj.size + 2 * own_heads.size),
            transcendentals=sources * rows * HD,
        ),
        name="cross_attention",
    )(place, got, mine, other, proj, own_heads)


def self_attention_kernel(
    block_rows,
    block_keys,
    q_ref,
    k_ref,
    v_ref,
    out_ref,
    keys_t,
    values_x,
    scores,
    tops,
):
    chunk = q_ref.shape[1]
    length = k_ref.shape[0] * chunk
    key_blocks = length // block_keys
    query_blocks = length // block_rows
    for piece in range(length // chunk):
        keys_t[:, piece * chunk : (piece + 1) * chunk] = k_ref[piece].T
        values_x[piece * chunk : (piece + 1) * chunk, :HD] = v_ref[piece]
    values_x[:, HD:] = jnp.ones((length, HD), BF16)
    per_block = block_rows // chunk

    def queries_of(block):
        rows = q_ref[pl.ds(block * per_block, per_block)]
        return rows.reshape(block_rows, HD)

    def highest(top, part):
        for group in range(part.shape[1] // HD):
            lanes = part[:, group * HD : (group + 1) * HD]
            top = lanes if top is None else jnp.maximum(top, lanes)
        return top

    def row_max(top):
        return jnp.broadcast_to(jnp.max(top, axis=1, keepdims=True), (block_rows, HD))

    first = queries_of(0)
    top = None
    for j in range(key_blocks):
        keys = slice(j * block_keys, (j + 1) * block_keys)
        part = jnp.dot(first, keys_t[:, keys], preferred_element_type=F32)
        scores[0, :, keys] = part
        top = highest(top, part)
    tops[0] = row_max(top)

    def body(i, carry):
        slot = lax.rem(i, 2)
        later = 1 - slot
        queries = queries_of(jnp.minimum(i + 1, query_blocks - 1))
        top_here = tops[slot][:, :1]
        top = None
        total = None
        for j in range(key_blocks):
            keys = slice(j * block_keys, (j + 1) * block_keys)
            part = jnp.dot(queries, keys_t[:, keys], preferred_element_type=F32)
            scores[later, :, keys] = part
            top = highest(top, part)
            raised = jnp.exp2((scores[slot, :, keys] - top_here) * EXP2_SCALING).astype(BF16)
            mixed = jnp.dot(raised, values_x[keys, :], preferred_element_type=F32)
            total = mixed if total is None else total + mixed
        tops[later] = row_max(top)
        own = (total[:, :HD] / total[:, HD:]).astype(BF16)
        out_ref[pl.ds(i * per_block, per_block)] = own.reshape(per_block, chunk, HD)
        return carry

    lax.fori_loop(0, query_blocks, body, 0)


def attend_self(qkv, rows):
    sources = qkv.shape[0]
    length = sources * rows
    block_rows, block_keys = 512, 512

    def whole(which):
        return pl.BlockSpec((sources, rows, HD), lambda i: (0, which, 0))

    flat = pl.BlockSpec((sources, rows, HD), lambda i: (0, 0, 0))
    return pl.pallas_call(
        functools.partial(self_attention_kernel, block_rows, block_keys),
        grid=(1,),
        in_specs=[whole(0), whole(1), whole(2)],
        out_specs=flat,
        out_shape=jax.ShapeDtypeStruct((sources, rows, HD), BF16),
        scratch_shapes=[
            pltpu.VMEM((HD, length), BF16),
            pltpu.VMEM((length, 2 * HD), BF16),
            pltpu.VMEM((2, block_rows, length), F32),
            pltpu.VMEM((2, block_rows, HD), F32),
        ],
        compiler_params=kernel_params(),
        cost_estimate=pl.CostEstimate(
            flops=8 * length * length * HD,
            bytes_accessed=8 * length * HD,
            transcendentals=length * length,
        ),
        name="self_attention",
    )(qkv, qkv, qkv)


def arrive_kernel(group, owned, got_ref, out_ref, sum_ref, total):
    rows = out_ref.shape[0]
    for head in range(group):
        out_ref[:, head * HD : (head + 1) * HD] = got_ref[head, 0:rows]

    @pl.when(pl.program_id(0) == 0)
    def _():
        total[...] = jnp.zeros_like(total)

    total[...] += jnp.sum(got_ref[:, rows:].astype(F32), axis=0)
    for chunk in range(total.shape[0] // owned):
        sum_ref[:, chunk * HD : (chunk + 1) * HD] = total[chunk * owned : (chunk + 1) * owned]


def arrived(got, rows, owned):
    heads, total, _ = got.shape
    features = (total - rows) // owned * HD
    group = 8
    return pl.pallas_call(
        functools.partial(arrive_kernel, group, owned),
        grid=(heads // group,),
        in_specs=[pl.BlockSpec((group, total, HD), lambda i: (i, 0, 0))],
        out_specs=[
            pl.BlockSpec((None, rows, group * HD), lambda i: (0, 0, i)),
            pl.BlockSpec((None, owned, features), lambda i: (0, 0, 0)),
        ],
        out_shape=[
            jax.ShapeDtypeStruct((1, rows, heads * HD), BF16),
            jax.ShapeDtypeStruct((1, owned, features), F32),
        ],
        scratch_shapes=[pltpu.VMEM((total - rows, HD), F32)],
        compiler_params=kernel_params(),
        cost_estimate=pl.CostEstimate(
            flops=got.size, bytes_accessed=4 * got.size, transcendentals=0
        ),
        name="arrived",
    )(got)


def local(
    self_q,
    self_k,
    self_v,
    cross_q,
    audio,
    key_weight,
    value_weight,
    intersection,
    counts,
    cotangent,
):
    here = lax.axis_index("seq")
    core = lax.rem(here, 2)
    rows = self_q.shape[1]
    owned, features = audio.shape[1:]

    qkv = self_heads(self_q, self_k, self_v, audio)
    qkv, cross_q, key_weight, value_weight = lax.optimization_barrier(
        (qkv, cross_q, key_weight, value_weight)
    )
    qkv = handed_over(qkv)

    band_first = (here * (owned // AB) - REACH)[None].astype(jnp.int32)
    cross = cross_heads(intersection[0], counts[0], band_first, cross_q, cotangent)
    both = jnp.concatenate([key_weight, value_weight], axis=1)
    proj = gathered_by_doubling(both[None], "fsdp").reshape(-1, 2 * HD)
    place = jnp.stack([core, 1 - core]).astype(jnp.int32) * (features // 2)
    qkv, cross, proj, place = lax.optimization_barrier((qkv, cross, proj, place))

    cross = handed_over(cross)
    mine = qkv[:, 3 * rows :]
    other = from_other_core(mine)
    own_heads = attend_self(qkv, rows)
    sent = cross_attention(place, cross, mine, other, proj, own_heads)
    block_out, audio_grad = arrived(handed_over(sent), rows, owned)
    return (block_out, audio_grad)


def solution(mesh):
    in_specs = (
        P("fsdp", "seq", None),
        P("fsdp", "seq", None),
        P("fsdp", "seq", None),
        P("fsdp", "seq", None),
        P("fsdp", "seq", None),
        P("fsdp", "seq"),
        P("fsdp", "seq"),
        P("fsdp", "seq", None),
        P("fsdp", "seq"),
        P("fsdp", "seq", None),
    )
    out_specs = (P("fsdp", "seq", None), P("fsdp", "seq", None))
    return jax.shard_map(local, mesh=mesh, in_specs=in_specs, out_specs=out_specs, check_vma=False)
```

```python
import functools

import jax
import jax.numpy as jnp
from jax import lax
from jax.experimental import pallas as pl
from jax.experimental.pallas import tpu as pltpu
from jax.sharding import PartitionSpec as P

HD = 128
AB = 16
REACH = 3
PAD = 16
SCALING = HD ** (-0.5)
EXP2_SCALING = SCALING * 1.4426950408889634
F32 = jnp.float32
BF16 = jnp.bfloat16
MIB = 1024 * 1024


def kernel_params(mib=48):
    return pltpu.CompilerParams(vmem_limit_bytes=mib * MIB)


def handed_over(parts):
    return lax.all_to_all(parts, "seq", split_axis=0, concat_axis=0, tiled=True)


def gathered_by_doubling(block, axis):
    size = lax.axis_size(axis)
    here = lax.axis_index(axis)
    step = 1
    while step < size:
        other = lax.ppermute(block, axis, [(i, i ^ step) for i in range(size)])
        upper = (here & step) != 0
        block = jnp.concatenate(
            [jnp.where(upper, other, block), jnp.where(upper, block, other)], axis=0
        )
        step *= 2
    return block


def from_other_core(block):
    size = lax.axis_size("seq")
    return lax.ppermute(block, "seq", [(i, i ^ 1) for i in range(size)])


def contract(a, b, dim_a, dim_b):
    return lax.dot_general(a, b, (((dim_a,), (dim_b,)), ((), ())), preferred_element_type=F32)


def self_heads_kernel(group, q_ref, k_ref, v_ref, audio_ref, out_ref):
    rows = q_ref.shape[0]
    owned, features = audio_ref.shape
    chunks = features // HD // 2
    for head in range(group):
        cols = slice(head * HD, (head + 1) * HD)
        out_ref[head, 0:rows] = q_ref[:, cols]
        out_ref[head, rows : 2 * rows] = k_ref[:, cols]
        out_ref[head, 2 * rows : 3 * rows] = v_ref[:, cols]
        for chunk in range(chunks):
            first = 3 * rows + chunk * owned
            lane = (head % 2 * chunks + chunk) * HD
            out_ref[head, first : first + owned] = audio_ref[:, lane : lane + HD]


def self_heads(q_local, k_local, v_local, audio):
    _, rows, width = q_local.shape
    _, owned, features = audio.shape
    heads = width // HD
    group = 8
    total = 3 * rows + owned * (features // HD // 2)
    block = pl.BlockSpec((None, rows, group * HD), lambda i: (0, 0, i))
    return pl.pallas_call(
        functools.partial(self_heads_kernel, group),
        grid=(heads // group,),
        in_specs=[block] * 3 + [pl.BlockSpec((None, owned, features), lambda i: (0, 0, 0))],
        out_specs=pl.BlockSpec((group, total, HD), lambda i: (i, 0, 0)),
        out_shape=jax.ShapeDtypeStruct((heads, total, HD), BF16),
        compiler_params=kernel_params(60),
        cost_estimate=pl.CostEstimate(
            flops=0, bytes_accessed=7 * rows * width * 2, transcendentals=0
        ),
        name="self_heads",
    )(q_local, k_local, v_local, audio)


def cross_heads_kernel(group, ids_ref, counts_ref, first_ref, q_ref, grad_ref, out_ref):
    rows = q_ref.shape[0]
    frames, slots = ids_ref.shape
    blocks = first_ref[0] + lax.broadcasted_iota(jnp.int32, (PAD, HD), 1) // AB
    row = lax.broadcasted_iota(jnp.int32, (PAD, HD), 0)
    live = jnp.zeros((PAD, HD), F32)
    for frame in range(frames):
        for slot in range(slots):
            hit = (blocks == ids_ref[frame, slot]) & (row == frame)
            hit = hit & (counts_ref[frame] > slot)
            live = jnp.where(hit, 1.0, live)
    live = live.astype(BF16)
    for head in range(group):
        cols = slice(head * HD, (head + 1) * HD)
        out_ref[head, 0:rows] = q_ref[:, cols]
        out_ref[head, rows : 2 * rows] = grad_ref[:, cols]
        out_ref[head, 2 * rows :] = live


def cross_heads(window_ids, live_counts, band_first, queries, grads):
    _, rows, width = queries.shape
    heads = width // HD
    group = 8
    total = 2 * rows + PAD
    block = pl.BlockSpec((None, rows, group * HD), lambda i: (0, 0, i))
    scalars = pl.BlockSpec(memory_space=pltpu.SMEM)
    return pl.pallas_call(
        functools.partial(cross_heads_kernel, group),
        grid=(heads // group,),
        in_specs=[scalars, scalars, scalars, block, block],
        out_specs=pl.BlockSpec((group, total, HD), lambda i: (i, 0, 0)),
        out_shape=jax.ShapeDtypeStruct((heads, total, HD), BF16),
        compiler_params=kernel_params(60),
        cost_estimate=pl.CostEstimate(
            flops=0, bytes_accessed=4 * rows * width * 2, transcendentals=0
        ),
        name="cross_heads",
    )(window_ids, live_counts, band_first, queries, grads)


def project_kernel(
    audio_first, place_ref, qkv_ref, other_ref, proj_ref, keys_ref, values_ref, audio, sem
):
    sources, owned, features = audio.shape
    chunks = features // HD // 2
    length = sources * owned
    edge = REACH * AB
    copies = []
    for chunk in range(chunks):
        for kind, (ref, first) in enumerate(((qkv_ref, audio_first), (other_ref, 0))):
            lanes = pl.ds(pl.multiple_of(place_ref[kind] + chunk * HD, HD), HD)
            copies.append(
                pltpu.make_async_copy(
                    ref.at[:, pl.ds(first + chunk * owned, owned), :],
                    audio.at[:, :, lanes],
                    sem.at[kind, chunk],
                )
            )
            copies[-1].start()
    tail = keys_ref.shape[0] - edge - length
    for ref in (keys_ref, values_ref):
        ref[0:edge] = jnp.zeros((edge, HD), BF16)
        ref[edge + length :] = jnp.zeros((tail, HD), BF16)
    for copy in copies:
        copy.wait()
    step = 256
    per = step // owned
    for i in range(length // step):
        rows = audio[i * per : (i + 1) * per].reshape(step, features)
        both = jnp.dot(rows, proj_ref[...], preferred_element_type=F32).astype(BF16)
        keys_ref[edge + i * step : edge + (i + 1) * step] = both[:, :HD]
        values_ref[edge + i * step : edge + (i + 1) * step] = both[:, HD:]


def projected(place, qkv, audio_first, other, proj):
    sources, audio_rows, _ = other.shape
    features = proj.shape[0]
    owned = 2 * AB
    length = sources * owned
    padded = length + HD - owned
    anywhere = pl.BlockSpec(memory_space=pl.ANY)
    flat = pl.BlockSpec((padded, HD), lambda i: (0, 0))
    return pl.pallas_call(
        functools.partial(project_kernel, audio_first),
        grid=(1,),
        in_specs=[
            pl.BlockSpec(memory_space=pltpu.SMEM),
            anywhere,
            anywhere,
            pl.BlockSpec((features, 2 * HD), lambda i: (0, 0)),
        ],
        out_specs=[flat, flat],
        out_shape=[jax.ShapeDtypeStruct((padded, HD), BF16)] * 2,
        scratch_shapes=[
            pltpu.VMEM((sources, owned, features), BF16),
            pltpu.SemaphoreType.DMA((2, features // HD // 2)),
        ],
        compiler_params=kernel_params(16),
        cost_estimate=pl.CostEstimate(
            flops=4 * length * features * HD,
            bytes_accessed=2 * (length * features + proj.size + 2 * padded * HD),
            transcendentals=0,
        ),
        name="projected",
    )(place, qkv, other, proj)


def cross_kernel(
    rows,
    place_ref,
    got_hbm,
    own_hbm,
    keys_ref,
    values_ref,
    proj_ref,
    sent_hbm,
    away_hbm,
    got,
    own,
    out,
    terms,
    away,
    d_keys,
    d_values,
    in_sem,
    out_sem,
):
    sources = got.shape[0]
    owned = AB * 2
    features = proj_ref.shape[0]
    half = features // 2
    chunks = half // HD
    length = sources * owned
    edge = REACH * AB
    band = HD
    at_once = 8
    blocks = sources // at_once

    fetched = []
    for block in range(blocks):
        here = pl.ds(block * at_once, at_once)
        pair = (
            pltpu.make_async_copy(got_hbm.at[here], got.at[here], in_sem.at[0, block]),
            pltpu.make_async_copy(own_hbm.at[here], own.at[here], in_sem.at[1, block]),
        )
        for copy in pair:
            copy.start()
        fetched.append(pair)
    d_keys[...] = jnp.zeros_like(d_keys)
    d_values[...] = jnp.zeros_like(d_values)

    stored = []
    for block in range(blocks):
        for copy in fetched[block]:
            copy.wait()
        sources_here = [block * at_once + i for i in range(at_once)]
        bands = [slice(t * owned, t * owned + band) for t in sources_here]
        k = [keys_ref[b] for b in bands]
        v = [values_ref[b] for b in bands]
        scores = [contract(got[t, 0:rows], k[i], 1, 1) for i, t in enumerate(sources_here)]
        d_probs = [
            contract(got[t, rows : 2 * rows], v[i], 1, 1) for i, t in enumerate(sources_here)
        ]
        weights = []
        for i, t in enumerate(sources_here):
            masks = got[t, 2 * rows :].astype(F32)
            live = jnp.concatenate(
                [jnp.broadcast_to(masks[f : f + 1], (rows // 2, band)) for f in range(2)], axis=0
            )
            masked = jnp.where(live > 0, scores[i], -1e30)
            top = jnp.max(masked, axis=1, keepdims=True)
            raised = jnp.exp2((masked - top) * EXP2_SCALING)
            weights.append(raised / jnp.sum(raised, axis=1, keepdims=True))
        weights_b = [part.astype(BF16) for part in weights]
        d_scores = []
        for i in range(at_once):
            weighed = weights[i] * d_probs[i]
            inner = jnp.sum(weighed, axis=1, keepdims=True)
            d_scores.append((weighed - weights[i] * inner).astype(BF16))
        for i, t in enumerate(sources_here):
            mixed = jnp.dot(weights_b[i], v[i], preferred_element_type=F32)
            out[t] = (own[t].astype(F32) + mixed).astype(BF16)
        for i, t in enumerate(sources_here):
            d_values[bands[i]] += contract(weights_b[i], got[t, rows : 2 * rows], 0, 0)
            d_keys[bands[i]] += contract(d_scores[i], got[t, 0:rows], 0, 0)
        here = pl.ds(block * at_once, at_once)
        stored.append(
            pltpu.make_async_copy(
                out.at[here], sent_hbm.at[here, pl.ds(0, rows), :], out_sem.at[0, block]
            )
        )
        stored[-1].start()

    own_proj = proj_ref[pl.ds(pl.multiple_of(place_ref[0], HD), half)]
    other_proj = proj_ref[pl.ds(pl.multiple_of(place_ref[1], HD), half)]
    step = length // blocks
    per = step // owned
    for block in range(blocks):
        rows_here = slice(edge + block * step, edge + (block + 1) * step)
        d_both = jnp.concatenate(
            [(d_keys[rows_here] * SCALING).astype(BF16), d_values[rows_here].astype(BF16)], axis=1
        )
        for buffer, part in ((away, other_proj), (terms, own_proj)):
            term = contract(d_both, part, 1, 1).astype(BF16)
            for chunk in range(chunks):
                buffer[
                    block * per : (block + 1) * per, chunk * owned : (chunk + 1) * owned
                ] = term[:, chunk * HD : (chunk + 1) * HD].reshape(per, owned, HD)
        here = pl.ds(block * per, per)
        stored += [
            pltpu.make_async_copy(away.at[here], away_hbm.at[here], out_sem.at[1, block]),
            pltpu.make_async_copy(
                terms.at[here],
                sent_hbm.at[here, pl.ds(rows, chunks * owned), :],
                out_sem.at[2, block],
            ),
        ]
        for copy in stored[-2:]:
            copy.start()
    for copy in stored:
        copy.wait()


def cross_attention(place, got, own_heads, keys, values, proj):
    sources, rows, _ = own_heads.shape
    total = got.shape[1]
    features = proj.shape[0]
    owned = 2 * AB
    padded = keys.shape[0]
    term_rows = features // 2 // HD * owned
    anywhere = pl.BlockSpec(memory_space=pl.ANY)
    flat = pl.BlockSpec((padded, HD), lambda i: (0, 0))
    return pl.pallas_call(
        functools.partial(cross_kernel, rows),
        grid=(1,),
        in_specs=[
            pl.BlockSpec(memory_space=pltpu.SMEM),
            anywhere,
            anywhere,
            flat,
            flat,
            pl.BlockSpec((features, 2 * HD), lambda i: (0, 0)),
        ],
        out_specs=[anywhere, anywhere],
        out_shape=[
            jax.ShapeDtypeStruct((sources, rows + term_rows, HD), BF16),
            jax.ShapeDtypeStruct((sources, term_rows, HD), BF16),
        ],
        scratch_shapes=[
            pltpu.VMEM((sources, total, HD), BF16),
            pltpu.VMEM((sources, rows, HD), BF16),
            pltpu.VMEM((sources, rows, HD), BF16),
            pltpu.VMEM((sources, term_rows, HD), BF16),
            pltpu.VMEM((sources, term_rows, HD), BF16),
            pltpu.VMEM((padded, HD), F32),
            pltpu.VMEM((padded, HD), F32),
            pltpu.SemaphoreType.DMA((2, sources // 8)),
            pltpu.SemaphoreType.DMA((3, sources // 8)),
        ],
        compiler_params=kernel_params(60),
        cost_estimate=pl.CostEstimate(
            flops=4 * sources * owned * features * HD + 10 * sources * rows * HD * HD,
            bytes_accessed=2 * (got.size + proj.size + 4 * own_heads.size),
            transcendentals=sources * rows * HD,
        ),
        name="cross_attention",
    )(place, got, own_heads, keys, values, proj)


def pair_kernel(sent_ref, came_ref, out_ref):
    out_ref[...] = (sent_ref[...].astype(F32) + came_ref[...].astype(F32)).astype(BF16)


def pair_added(sent, came):
    sources, term_rows, _ = came.shape
    total = sent.shape[1]
    width = 32
    ahead = (total - term_rows) // width
    block = pl.BlockSpec((sources, width, HD), lambda i: (0, ahead + i, 0))
    return pl.pallas_call(
        pair_kernel,
        grid=(term_rows // width,),
        in_specs=[block, pl.BlockSpec((sources, width, HD), lambda i: (0, i, 0))],
        out_specs=block,
        out_shape=jax.ShapeDtypeStruct(sent.shape, BF16),
        input_output_aliases={0: 0},
        compiler_params=kernel_params(8),
        cost_estimate=pl.CostEstimate(
            flops=came.size, bytes_accessed=6 * came.size, transcendentals=0
        ),
        name="pair_added",
    )(sent, came)


def self_attention_kernel(
    block_rows,
    block_keys,
    unrolled,
    q_ref,
    k_ref,
    v_ref,
    out_ref,
    keys_t,
    values_x,
    scores,
    tops,
):
    chunk = q_ref.shape[1]
    length = k_ref.shape[0] * chunk
    key_blocks = length // block_keys
    query_blocks = length // block_rows
    for piece in range(length // chunk):
        keys_t[:, piece * chunk : (piece + 1) * chunk] = k_ref[piece].T
        values_x[piece * chunk : (piece + 1) * chunk, :HD] = v_ref[piece]
    values_x[:, HD:] = jnp.ones((length, HD), BF16)
    per_block = block_rows // chunk

    def queries_of(block):
        rows = q_ref[pl.ds(block * per_block, per_block)]
        return rows.reshape(block_rows, HD)

    def highest(top, part):
        for group in range(part.shape[1] // HD):
            lanes = part[:, group * HD : (group + 1) * HD]
            top = lanes if top is None else jnp.maximum(top, lanes)
        return top

    def row_max(top):
        return jnp.broadcast_to(jnp.max(top, axis=1, keepdims=True), (block_rows, HD))

    first = queries_of(0)
    top = None
    for j in range(key_blocks):
        keys = slice(j * block_keys, (j + 1) * block_keys)
        part = jnp.dot(first, keys_t[:, keys], preferred_element_type=F32)
        scores[0, :, keys] = part
        top = highest(top, part)
    tops[0] = row_max(top)

    def one(block, slot, later):
        queries = queries_of(jnp.minimum(block + 1, query_blocks - 1))
        top_here = tops[slot][:, :1]
        top = None
        total = None
        for j in range(key_blocks):
            keys = slice(j * block_keys, (j + 1) * block_keys)
            part = jnp.dot(queries, keys_t[:, keys], preferred_element_type=F32)
            scores[later, :, keys] = part
            top = highest(top, part)
            raised = jnp.exp2((scores[slot, :, keys] - top_here) * EXP2_SCALING).astype(BF16)
            mixed = jnp.dot(raised, values_x[keys, :], preferred_element_type=F32)
            total = mixed if total is None else total + mixed
        tops[later] = row_max(top)
        own = (total[:, :HD] / total[:, HD:]).astype(BF16)
        out_ref[pl.ds(block * per_block, per_block)] = own.reshape(per_block, chunk, HD)

    def body(i, carry):
        for u in range(unrolled):
            one(i * unrolled + u, u % 2, 1 - u % 2)
        return carry

    lax.fori_loop(0, query_blocks // unrolled, body, 0)


def attend_self(qkv, rows):
    sources = qkv.shape[0]
    length = sources * rows
    block_rows, block_keys, unrolled = 512, 512, 4

    def whole(which):
        return pl.BlockSpec((sources, rows, HD), lambda i: (0, which, 0))

    flat = pl.BlockSpec((sources, rows, HD), lambda i: (0, 0, 0))
    return pl.pallas_call(
        functools.partial(self_attention_kernel, block_rows, block_keys, unrolled),
        grid=(1,),
        in_specs=[whole(0), whole(1), whole(2)],
        out_specs=flat,
        out_shape=jax.ShapeDtypeStruct((sources, rows, HD), BF16),
        scratch_shapes=[
            pltpu.VMEM((HD, length), BF16),
            pltpu.VMEM((length, 2 * HD), BF16),
            pltpu.VMEM((2, block_rows, length), F32),
            pltpu.VMEM((2, block_rows, HD), F32),
        ],
        compiler_params=kernel_params(60),
        cost_estimate=pl.CostEstimate(
            flops=8 * length * length * HD,
            bytes_accessed=8 * length * HD,
            transcendentals=length * length,
        ),
        name="self_attention",
    )(qkv, qkv, qkv)


def arrive_kernel(group, owned, got_ref, out_ref, sum_ref, total):
    rows = out_ref.shape[0]
    for head in range(group):
        out_ref[:, head * HD : (head + 1) * HD] = got_ref[head, 0:rows]

    @pl.when(pl.program_id(0) == 0)
    def _():
        total[...] = jnp.zeros_like(total)

    chunks = total.shape[1] // owned
    for core in range(2):
        part = total[core]
        for head in range(core, group, 2):
            part = part + got_ref[head, rows:].astype(F32)
        total[core] = part

    @pl.when(pl.program_id(0) == pl.num_programs(0) - 1)
    def _():
        for core in range(2):
            for chunk in range(chunks):
                lane = (core * chunks + chunk) * HD
                sum_ref[:, lane : lane + HD] = total[core, chunk * owned : (chunk + 1) * owned]


def arrived(got, rows, owned):
    heads, total, _ = got.shape
    features = 2 * (total - rows) // owned * HD
    group = 8
    return pl.pallas_call(
        functools.partial(arrive_kernel, group, owned),
        grid=(heads // group,),
        in_specs=[pl.BlockSpec((group, total, HD), lambda i: (i, 0, 0))],
        out_specs=[
            pl.BlockSpec((None, rows, group * HD), lambda i: (0, 0, i)),
            pl.BlockSpec((None, owned, features), lambda i: (0, 0, 0)),
        ],
        out_shape=[
            jax.ShapeDtypeStruct((1, rows, heads * HD), BF16),
            jax.ShapeDtypeStruct((1, owned, features), F32),
        ],
        scratch_shapes=[pltpu.VMEM((2, total - rows, HD), F32)],
        compiler_params=kernel_params(16),
        cost_estimate=pl.CostEstimate(
            flops=got.size, bytes_accessed=4 * got.size, transcendentals=0
        ),
        name="arrived",
    )(got)


def local(
    self_q,
    self_k,
    self_v,
    cross_q,
    audio,
    key_weight,
    value_weight,
    intersection,
    counts,
    cotangent,
):
    here = lax.axis_index("seq")
    core = lax.rem(here, 2)
    rows = self_q.shape[1]
    owned, features = audio.shape[1:]

    qkv = self_heads(self_q, self_k, self_v, audio)
    qkv, cross_q, key_weight, value_weight = lax.optimization_barrier(
        (qkv, cross_q, key_weight, value_weight)
    )
    qkv = handed_over(qkv)

    band_first = (here * (owned // AB) - REACH)[None].astype(jnp.int32)
    cross = cross_heads(intersection[0], counts[0], band_first, cross_q, cotangent)
    both = jnp.concatenate([key_weight, value_weight], axis=1)
    proj = gathered_by_doubling(both[None], "fsdp").reshape(-1, 2 * HD)
    place = jnp.stack([core, 1 - core]).astype(jnp.int32) * (features // 2)
    qkv, cross, proj, place = lax.optimization_barrier((qkv, cross, proj, place))

    cross = handed_over(cross)
    other = from_other_core(qkv[:, 3 * rows :])
    own_heads = attend_self(qkv, rows)
    keys, values = projected(place, qkv, 3 * rows, other, proj)
    sent, away = cross_attention(place, cross, own_heads, keys, values, proj)
    sent = pair_added(sent, from_other_core(away))
    block_out, audio_grad = arrived(handed_over(sent), rows, owned)
    return (block_out, audio_grad)


def solution(mesh):
    in_specs = (
        P("fsdp", "seq", None),
        P("fsdp", "seq", None),
        P("fsdp", "seq", None),
        P("fsdp", "seq", None),
        P("fsdp", "seq", None),
        P("fsdp", "seq"),
        P("fsdp", "seq"),
        P("fsdp", "seq", None),
        P("fsdp", "seq"),
        P("fsdp", "seq", None),
    )
    out_specs = (P("fsdp", "seq", None), P("fsdp", "seq", None))
    return jax.shard_map(local, mesh=mesh, in_specs=in_specs, out_specs=out_specs, check_vma=False)
```

```python
import functools

import jax
import jax.numpy as jnp
from jax import lax
from jax.experimental import pallas as pl
from jax.experimental.pallas import tpu as pltpu
from jax.sharding import PartitionSpec as P

HD = 128
AB = 16
REACH = 3
PAD = 16
SCALING = HD ** (-0.5)
EXP2_SCALING = SCALING * 1.4426950408889634
F32 = jnp.float32
BF16 = jnp.bfloat16
MIB = 1024 * 1024


IN_HBM = pl.BlockSpec(memory_space=pltpu.HBM)


def kernel_params(mib=48):
    return pltpu.CompilerParams(vmem_limit_bytes=mib * MIB)


def handed_over(parts):
    return lax.all_to_all(parts, "seq", split_axis=0, concat_axis=0, tiled=True)


def gathered_by_doubling(block, axis):
    size = lax.axis_size(axis)
    here = lax.axis_index(axis)
    step = 1
    while step < size:
        other = lax.ppermute(block, axis, [(i, i ^ step) for i in range(size)])
        upper = (here & step) != 0
        block = jnp.concatenate(
            [jnp.where(upper, other, block), jnp.where(upper, block, other)], axis=0
        )
        step *= 2
    return block


def from_other_core(block):
    size = lax.axis_size("seq")
    return lax.ppermute(block, "seq", [(i, i ^ 1) for i in range(size)])


def contract(a, b, dim_a, dim_b):
    return lax.dot_general(a, b, (((dim_a,), (dim_b,)), ((), ())), preferred_element_type=F32)


def self_heads_kernel(
    group, q_hbm, k_hbm, v_hbm, audio_hbm, out_hbm, loaded, audio, out, in_sem, audio_sem, out_sem
):
    heads = out.shape[0]
    rows = loaded.shape[1]
    owned, features = audio.shape
    chunks = features // HD // 2
    loads = []
    for first in range(0, heads, group):
        cols = pl.ds(first * HD, group * HD)
        part = [
            pltpu.make_async_copy(
                source.at[0, :, cols], loaded.at[which, :, cols], in_sem.at[which, first // group]
            )
            for which, source in enumerate((q_hbm, k_hbm, v_hbm))
        ]
        for copy in part:
            copy.start()
        loads.append(part)
    audio_load = pltpu.make_async_copy(audio_hbm.at[0], audio, audio_sem)
    audio_load.start()
    audio_load.wait()
    stores = []
    for part in range(len(loads)):
        for copy in loads[part]:
            copy.wait()
        for head in range(part * group, (part + 1) * group):
            for which in range(3):
                out[head, which * rows : (which + 1) * rows] = loaded[
                    which, :, head * HD : (head + 1) * HD
                ]
            for chunk in range(chunks):
                first = 3 * rows + chunk * owned
                lane = (head % 2 * chunks + chunk) * HD
                out[head, first : first + owned] = audio[:, lane : lane + HD]
        here = pl.ds(part * group, group)
        stores.append(pltpu.make_async_copy(out.at[here], out_hbm.at[here], out_sem.at[part]))
        stores[-1].start()
    for copy in stores:
        copy.wait()


def self_heads(q_local, k_local, v_local, audio):
    _, rows, width = q_local.shape
    _, owned, features = audio.shape
    heads = width // HD
    group = 4
    total = 3 * rows + owned * (features // HD // 2)
    return pl.pallas_call(
        functools.partial(self_heads_kernel, group),
        in_specs=[IN_HBM] * 4,
        out_specs=IN_HBM,
        out_shape=jax.ShapeDtypeStruct((heads, total, HD), BF16),
        scratch_shapes=[
            pltpu.VMEM((3, rows, width), BF16),
            pltpu.VMEM((owned, features), BF16),
            pltpu.VMEM((heads, total, HD), BF16),
            pltpu.SemaphoreType.DMA((3, heads // group)),
            pltpu.SemaphoreType.DMA,
            pltpu.SemaphoreType.DMA((heads // group,)),
        ],
        compiler_params=kernel_params(60),
        cost_estimate=pl.CostEstimate(
            flops=0, bytes_accessed=7 * rows * width * 2, transcendentals=0
        ),
        name="self_heads",
    )(q_local, k_local, v_local, audio)


def cross_heads_kernel(group, ids_ref, counts_ref, first_ref, q_ref, grad_ref, out_ref):
    rows = q_ref.shape[0]
    frames, slots = ids_ref.shape
    blocks = first_ref[0] + lax.broadcasted_iota(jnp.int32, (PAD, HD), 1) // AB
    row = lax.broadcasted_iota(jnp.int32, (PAD, HD), 0)
    live = jnp.zeros((PAD, HD), F32)
    for frame in range(frames):
        for slot in range(slots):
            hit = (blocks == ids_ref[frame, slot]) & (row == frame)
            hit = hit & (counts_ref[frame] > slot)
            live = jnp.where(hit, 1.0, live)
    live = live.astype(BF16)
    for head in range(group):
        cols = slice(head * HD, (head + 1) * HD)
        out_ref[head, 0:rows] = q_ref[:, cols]
        out_ref[head, rows : 2 * rows] = grad_ref[:, cols]
        out_ref[head, 2 * rows :] = live


def cross_heads(window_ids, live_counts, band_first, queries, grads):
    _, rows, width = queries.shape
    heads = width // HD
    group = 8
    total = 2 * rows + PAD
    block = pl.BlockSpec((None, rows, group * HD), lambda i: (0, 0, i))
    scalars = pl.BlockSpec(memory_space=pltpu.SMEM)
    return pl.pallas_call(
        functools.partial(cross_heads_kernel, group),
        grid=(heads // group,),
        in_specs=[scalars, scalars, scalars, block, block],
        out_specs=pl.BlockSpec((group, total, HD), lambda i: (i, 0, 0)),
        out_shape=jax.ShapeDtypeStruct((heads, total, HD), BF16),
        compiler_params=kernel_params(60),
        cost_estimate=pl.CostEstimate(
            flops=0, bytes_accessed=4 * rows * width * 2, transcendentals=0
        ),
        name="cross_heads",
    )(window_ids, live_counts, band_first, queries, grads)


def project_kernel(
    audio_first, place_ref, qkv_ref, other_ref, proj_ref, keys_ref, values_ref, audio, sem
):
    sources, owned, features = audio.shape
    chunks = features // HD // 2
    length = sources * owned
    edge = REACH * AB
    copies = []
    for chunk in range(chunks):
        for kind, (ref, first) in enumerate(((qkv_ref, audio_first), (other_ref, 0))):
            lanes = pl.ds(pl.multiple_of(place_ref[kind] + chunk * HD, HD), HD)
            copies.append(
                pltpu.make_async_copy(
                    ref.at[:, pl.ds(first + chunk * owned, owned), :],
                    audio.at[:, :, lanes],
                    sem.at[kind, chunk],
                )
            )
            copies[-1].start()
    tail = keys_ref.shape[0] - edge - length
    for ref in (keys_ref, values_ref):
        ref[0:edge] = jnp.zeros((edge, HD), BF16)
        ref[edge + length :] = jnp.zeros((tail, HD), BF16)
    for copy in copies:
        copy.wait()
    step = 256
    per = step // owned
    for i in range(length // step):
        rows = audio[i * per : (i + 1) * per].reshape(step, features)
        both = jnp.dot(rows, proj_ref[...], preferred_element_type=F32).astype(BF16)
        keys_ref[edge + i * step : edge + (i + 1) * step] = both[:, :HD]
        values_ref[edge + i * step : edge + (i + 1) * step] = both[:, HD:]


def projected(place, qkv, audio_first, other, proj):
    sources, audio_rows, _ = other.shape
    features = proj.shape[0]
    owned = 2 * AB
    length = sources * owned
    padded = length + HD - owned
    anywhere = pl.BlockSpec(memory_space=pl.ANY)
    flat = pl.BlockSpec((padded, HD), lambda i: (0, 0))
    return pl.pallas_call(
        functools.partial(project_kernel, audio_first),
        grid=(1,),
        in_specs=[
            pl.BlockSpec(memory_space=pltpu.SMEM),
            anywhere,
            anywhere,
            pl.BlockSpec((features, 2 * HD), lambda i: (0, 0)),
        ],
        out_specs=[flat, flat],
        out_shape=[jax.ShapeDtypeStruct((padded, HD), BF16)] * 2,
        scratch_shapes=[
            pltpu.VMEM((sources, owned, features), BF16),
            pltpu.SemaphoreType.DMA((2, features // HD // 2)),
        ],
        compiler_params=kernel_params(16),
        cost_estimate=pl.CostEstimate(
            flops=4 * length * features * HD,
            bytes_accessed=2 * (length * features + proj.size + 2 * padded * HD),
            transcendentals=0,
        ),
        name="projected",
    )(place, qkv, other, proj)


def cross_kernel(
    rows,
    place_ref,
    got_hbm,
    own_hbm,
    keys_ref,
    values_ref,
    proj_ref,
    sent_hbm,
    terms_hbm,
    away_hbm,
    got,
    own,
    out,
    terms,
    away,
    d_keys,
    d_values,
    in_sem,
    out_sem,
):
    sources = got.shape[0]
    owned = AB * 2
    features = proj_ref.shape[0]
    half = features // 2
    chunks = half // HD
    length = sources * owned
    edge = REACH * AB
    band = HD
    at_once = 8
    blocks = sources // at_once

    fetched = []
    for block in range(blocks):
        here = pl.ds(block * at_once, at_once)
        pair = (
            pltpu.make_async_copy(got_hbm.at[here], got.at[here], in_sem.at[0, block]),
            pltpu.make_async_copy(own_hbm.at[here], own.at[here], in_sem.at[1, block]),
        )
        for copy in pair:
            copy.start()
        fetched.append(pair)
    d_keys[...] = jnp.zeros_like(d_keys)
    d_values[...] = jnp.zeros_like(d_values)

    stored = []
    for block in range(blocks):
        for copy in fetched[block]:
            copy.wait()
        sources_here = [block * at_once + i for i in range(at_once)]
        bands = [slice(t * owned, t * owned + band) for t in sources_here]
        k = [keys_ref[b] for b in bands]
        v = [values_ref[b] for b in bands]
        scores = [contract(got[t, 0:rows], k[i], 1, 1) for i, t in enumerate(sources_here)]
        d_probs = [
            contract(got[t, rows : 2 * rows], v[i], 1, 1) for i, t in enumerate(sources_here)
        ]
        weights = []
        for i, t in enumerate(sources_here):
            masks = got[t, 2 * rows :].astype(F32)
            live = jnp.concatenate(
                [jnp.broadcast_to(masks[f : f + 1], (rows // 2, band)) for f in range(2)], axis=0
            )
            masked = jnp.where(live > 0, scores[i], -1e30)
            top = jnp.max(masked, axis=1, keepdims=True)
            raised = jnp.exp2((masked - top) * EXP2_SCALING)
            weights.append(raised / jnp.sum(raised, axis=1, keepdims=True))
        weights_b = [part.astype(BF16) for part in weights]
        d_scores = []
        for i in range(at_once):
            weighed = weights[i] * d_probs[i]
            inner = jnp.sum(weighed, axis=1, keepdims=True)
            d_scores.append((weighed - weights[i] * inner).astype(BF16))
        for i, t in enumerate(sources_here):
            mixed = jnp.dot(weights_b[i], v[i], preferred_element_type=F32)
            out[t] = (own[t].astype(F32) + mixed).astype(BF16)
        for i, t in enumerate(sources_here):
            d_values[bands[i]] += contract(weights_b[i], got[t, rows : 2 * rows], 0, 0)
            d_keys[bands[i]] += contract(d_scores[i], got[t, 0:rows], 0, 0)
        here = pl.ds(block * at_once, at_once)
        stored.append(
            pltpu.make_async_copy(
                out.at[here], sent_hbm.at[here, pl.ds(0, rows), :], out_sem.at[0, block]
            )
        )
        stored[-1].start()

    own_proj = proj_ref[pl.ds(pl.multiple_of(place_ref[0], HD), half)]
    other_proj = proj_ref[pl.ds(pl.multiple_of(place_ref[1], HD), half)]
    step = length // blocks
    per = step // owned
    for block in range(blocks):
        rows_here = slice(edge + block * step, edge + (block + 1) * step)
        d_both = jnp.concatenate(
            [(d_keys[rows_here] * SCALING).astype(BF16), d_values[rows_here].astype(BF16)], axis=1
        )
        for buffer, part in ((away, other_proj), (terms, own_proj)):
            term = contract(d_both, part, 1, 1).astype(BF16)
            for chunk in range(chunks):
                buffer[
                    block * per : (block + 1) * per, chunk * owned : (chunk + 1) * owned
                ] = term[:, chunk * HD : (chunk + 1) * HD].reshape(per, owned, HD)
        here = pl.ds(block * per, per)
        stored += [
            pltpu.make_async_copy(away.at[here], away_hbm.at[here], out_sem.at[1, block]),
            pltpu.make_async_copy(terms.at[here], terms_hbm.at[here], out_sem.at[2, block]),
        ]
        for copy in stored[-2:]:
            copy.start()
    for copy in stored:
        copy.wait()


def cross_attention(place, got, own_heads, keys, values, proj):
    sources, rows, _ = own_heads.shape
    total = got.shape[1]
    features = proj.shape[0]
    owned = 2 * AB
    padded = keys.shape[0]
    term_rows = features // 2 // HD * owned
    anywhere = pl.BlockSpec(memory_space=pl.ANY)
    flat = pl.BlockSpec((padded, HD), lambda i: (0, 0))
    term_shape = jax.ShapeDtypeStruct((sources, term_rows, HD), BF16)
    return pl.pallas_call(
        functools.partial(cross_kernel, rows),
        grid=(1,),
        in_specs=[
            pl.BlockSpec(memory_space=pltpu.SMEM),
            anywhere,
            anywhere,
            flat,
            flat,
            pl.BlockSpec((features, 2 * HD), lambda i: (0, 0)),
        ],
        out_specs=[anywhere, anywhere, anywhere],
        out_shape=[
            jax.ShapeDtypeStruct((sources, rows + term_rows, HD), BF16),
            term_shape,
            term_shape,
        ],
        scratch_shapes=[
            pltpu.VMEM((sources, total, HD), BF16),
            pltpu.VMEM((sources, rows, HD), BF16),
            pltpu.VMEM((sources, rows, HD), BF16),
            pltpu.VMEM((sources, term_rows, HD), BF16),
            pltpu.VMEM((sources, term_rows, HD), BF16),
            pltpu.VMEM((padded, HD), F32),
            pltpu.VMEM((padded, HD), F32),
            pltpu.SemaphoreType.DMA((2, sources // 8)),
            pltpu.SemaphoreType.DMA((3, sources // 8)),
        ],
        compiler_params=kernel_params(24),
        cost_estimate=pl.CostEstimate(
            flops=4 * sources * owned * features * HD + 10 * sources * rows * HD * HD,
            bytes_accessed=2 * (got.size + proj.size + 4 * own_heads.size),
            transcendentals=sources * rows * HD,
        ),
        name="cross_attention",
    )(place, got, own_heads, keys, values, proj)


def self_attention_kernel(
    block_rows,
    block_keys,
    unrolled,
    q_ref,
    k_ref,
    v_ref,
    out_ref,
    keys_t,
    values_x,
    scores,
    tops,
):
    chunk = q_ref.shape[1]
    length = k_ref.shape[0] * chunk
    key_blocks = length // block_keys
    query_blocks = length // block_rows
    for piece in range(length // chunk):
        keys_t[:, piece * chunk : (piece + 1) * chunk] = k_ref[piece].T
        values_x[piece * chunk : (piece + 1) * chunk, :HD] = v_ref[piece]
    values_x[:, HD:] = jnp.ones((length, HD), BF16)
    per_block = block_rows // chunk

    def queries_of(block):
        rows = q_ref[pl.ds(block * per_block, per_block)]
        return rows.reshape(block_rows, HD)

    def highest(top, part):
        for group in range(part.shape[1] // HD):
            lanes = part[:, group * HD : (group + 1) * HD]
            top = lanes if top is None else jnp.maximum(top, lanes)
        return top

    def row_max(top):
        return jnp.broadcast_to(jnp.max(top, axis=1, keepdims=True), (block_rows, HD))

    first = queries_of(0)
    top = None
    for j in range(key_blocks):
        keys = slice(j * block_keys, (j + 1) * block_keys)
        part = jnp.dot(first, keys_t[:, keys], preferred_element_type=F32)
        scores[0, :, keys] = part
        top = highest(top, part)
    tops[0] = row_max(top)

    def one(block, slot, later):
        queries = queries_of(jnp.minimum(block + 1, query_blocks - 1))
        top_here = tops[slot][:, :1]
        top = None
        total = None
        for j in range(key_blocks):
            keys = slice(j * block_keys, (j + 1) * block_keys)
            part = jnp.dot(queries, keys_t[:, keys], preferred_element_type=F32)
            scores[later, :, keys] = part
            top = highest(top, part)
            raised = jnp.exp2((scores[slot, :, keys] - top_here) * EXP2_SCALING).astype(BF16)
            mixed = jnp.dot(raised, values_x[keys, :], preferred_element_type=F32)
            total = mixed if total is None else total + mixed
        tops[later] = row_max(top)
        own = (total[:, :HD] / total[:, HD:]).astype(BF16)
        out_ref[pl.ds(block * per_block, per_block)] = own.reshape(per_block, chunk, HD)

    def body(i, carry):
        for u in range(unrolled):
            one(i * unrolled + u, u % 2, 1 - u % 2)
        return carry

    lax.fori_loop(0, query_blocks // unrolled, body, 0)


def attend_self(qkv, rows):
    sources = qkv.shape[0]
    length = sources * rows
    block_rows, block_keys, unrolled = 512, 512, 4

    def whole(which):
        return pl.BlockSpec((sources, rows, HD), lambda i: (0, which, 0))

    flat = pl.BlockSpec((sources, rows, HD), lambda i: (0, 0, 0))
    return pl.pallas_call(
        functools.partial(self_attention_kernel, block_rows, block_keys, unrolled),
        grid=(1,),
        in_specs=[whole(0), whole(1), whole(2)],
        out_specs=flat,
        out_shape=jax.ShapeDtypeStruct((sources, rows, HD), BF16),
        scratch_shapes=[
            pltpu.VMEM((HD, length), BF16),
            pltpu.VMEM((length, 2 * HD), BF16),
            pltpu.VMEM((2, block_rows, length), F32),
            pltpu.VMEM((2, block_rows, HD), F32),
        ],
        compiler_params=kernel_params(60),
        cost_estimate=pl.CostEstimate(
            flops=8 * length * length * HD,
            bytes_accessed=8 * length * HD,
            transcendentals=length * length,
        ),
        name="self_attention",
    )(qkv, qkv, qkv)


def arrive_kernel(group, owned, got_ref, out_ref, sum_ref, total):
    rows = out_ref.shape[0]
    for head in range(group):
        out_ref[:, head * HD : (head + 1) * HD] = got_ref[head, 0:rows]

    @pl.when(pl.program_id(0) == 0)
    def _():
        total[...] = jnp.zeros_like(total)

    chunks = total.shape[1] // owned
    for core in range(2):
        part = total[core]
        for head in range(core, group, 2):
            part = part + got_ref[head, rows:].astype(F32)
        total[core] = part

    @pl.when(pl.program_id(0) == pl.num_programs(0) - 1)
    def _():
        for core in range(2):
            for chunk in range(chunks):
                lane = (core * chunks + chunk) * HD
                sum_ref[:, lane : lane + HD] = total[core, chunk * owned : (chunk + 1) * owned]


def arrived(got, rows, owned):
    heads, total, _ = got.shape
    features = 2 * (total - rows) // owned * HD
    group = 8
    return pl.pallas_call(
        functools.partial(arrive_kernel, group, owned),
        grid=(heads // group,),
        in_specs=[pl.BlockSpec((group, total, HD), lambda i: (i, 0, 0))],
        out_specs=[
            pl.BlockSpec((None, rows, group * HD), lambda i: (0, 0, i)),
            pl.BlockSpec((None, owned, features), lambda i: (0, 0, 0)),
        ],
        out_shape=[
            jax.ShapeDtypeStruct((1, rows, heads * HD), BF16),
            jax.ShapeDtypeStruct((1, owned, features), F32),
        ],
        scratch_shapes=[pltpu.VMEM((2, total - rows, HD), F32)],
        compiler_params=kernel_params(16),
        cost_estimate=pl.CostEstimate(
            flops=got.size, bytes_accessed=4 * got.size, transcendentals=0
        ),
        name="arrived",
    )(got)


def local(
    self_q,
    self_k,
    self_v,
    cross_q,
    audio,
    key_weight,
    value_weight,
    intersection,
    counts,
    cotangent,
):
    here = lax.axis_index("seq")
    core = lax.rem(here, 2)
    rows = self_q.shape[1]
    owned, features = audio.shape[1:]

    qkv = self_heads(self_q, self_k, self_v, audio)
    qkv, cross_q, key_weight, value_weight = lax.optimization_barrier(
        (qkv, cross_q, key_weight, value_weight)
    )
    qkv = handed_over(qkv)

    band_first = (here * (owned // AB) - REACH)[None].astype(jnp.int32)
    cross = cross_heads(intersection[0], counts[0], band_first, cross_q, cotangent)
    both = jnp.concatenate([key_weight, value_weight], axis=1)
    proj = gathered_by_doubling(both[None], "fsdp").reshape(-1, 2 * HD)
    place = jnp.stack([core, 1 - core]).astype(jnp.int32) * (features // 2)
    qkv, cross, proj, place = lax.optimization_barrier((qkv, cross, proj, place))

    cross = handed_over(cross)
    other = from_other_core(qkv[:, 3 * rows :])
    own_heads = attend_self(qkv, rows)
    keys, values = projected(place, qkv, 3 * rows, other, proj)
    sent, terms, away = cross_attention(place, cross, own_heads, keys, values, proj)
    both_terms = terms.astype(F32) + from_other_core(away).astype(F32)
    sent = lax.dynamic_update_slice(sent, both_terms.astype(BF16), (0, rows, 0))
    block_out, audio_grad = arrived(handed_over(sent), rows, owned)
    return (block_out, audio_grad)


def solution(mesh):
    in_specs = (
        P("fsdp", "seq", None),
        P("fsdp", "seq", None),
        P("fsdp", "seq", None),
        P("fsdp", "seq", None),
        P("fsdp", "seq", None),
        P("fsdp", "seq"),
        P("fsdp", "seq"),
        P("fsdp", "seq", None),
        P("fsdp", "seq"),
        P("fsdp", "seq", None),
    )
    out_specs = (P("fsdp", "seq", None), P("fsdp", "seq", None))
    return jax.shard_map(local, mesh=mesh, in_specs=in_specs, out_specs=out_specs, check_vma=False)
```

```python
import functools

import jax
import jax.numpy as jnp
from jax import lax
from jax.experimental import pallas as pl
from jax.experimental.pallas import tpu as pltpu
from jax.sharding import PartitionSpec as P

HD = 128
AB = 16
REACH = 3
PAD = 16
SCALING = HD ** (-0.5)
EXP2_SCALING = SCALING * 1.4426950408889634
F32 = jnp.float32
BF16 = jnp.bfloat16
MIB = 1024 * 1024


IN_HBM = pl.BlockSpec(memory_space=pltpu.HBM)


def kernel_params(mib=48):
    return pltpu.CompilerParams(vmem_limit_bytes=mib * MIB)


def handed_over(parts):
    return lax.all_to_all(parts, "seq", split_axis=0, concat_axis=0, tiled=True)


def gathered_by_doubling(block, axis):
    size = lax.axis_size(axis)
    here = lax.axis_index(axis)
    step = 1
    while step < size:
        other = lax.ppermute(block, axis, [(i, i ^ step) for i in range(size)])
        upper = (here & step) != 0
        block = jnp.concatenate(
            [jnp.where(upper, other, block), jnp.where(upper, block, other)], axis=0
        )
        step *= 2
    return block


def from_other_core(block):
    size = lax.axis_size("seq")
    return lax.ppermute(block, "seq", [(i, i ^ 1) for i in range(size)])


def contract(a, b, dim_a, dim_b):
    return lax.dot_general(a, b, (((dim_a,), (dim_b,)), ((), ())), preferred_element_type=F32)


def self_heads_kernel(
    group, q_hbm, k_hbm, v_hbm, audio_hbm, out_hbm, loaded, audio, out, in_sem, audio_sem, out_sem
):
    heads = out.shape[0]
    rows = loaded.shape[1]
    owned, features = audio.shape
    chunks = features // HD // 2
    loads = []
    for first in range(0, heads, group):
        cols = pl.ds(first * HD, group * HD)
        part = [
            pltpu.make_async_copy(
                source.at[0, :, cols], loaded.at[which, :, cols], in_sem.at[which, first // group]
            )
            for which, source in enumerate((q_hbm, k_hbm, v_hbm))
        ]
        for copy in part:
            copy.start()
        loads.append(part)
    audio_load = pltpu.make_async_copy(audio_hbm.at[0], audio, audio_sem)
    audio_load.start()
    audio_load.wait()
    stores = []
    for part in range(len(loads)):
        for copy in loads[part]:
            copy.wait()
        for head in range(part * group, (part + 1) * group):
            for which in range(3):
                out[head, which * rows : (which + 1) * rows] = loaded[
                    which, :, head * HD : (head + 1) * HD
                ]
            for chunk in range(chunks):
                first = 3 * rows + chunk * owned
                lane = (head % 2 * chunks + chunk) * HD
                out[head, first : first + owned] = audio[:, lane : lane + HD]
        here = pl.ds(part * group, group)
        stores.append(pltpu.make_async_copy(out.at[here], out_hbm.at[here], out_sem.at[part]))
        stores[-1].start()
    for copy in stores:
        copy.wait()


def self_heads(q_local, k_local, v_local, audio):
    _, rows, width = q_local.shape
    _, owned, features = audio.shape
    heads = width // HD
    group = 4
    total = 3 * rows + owned * (features // HD // 2)
    return pl.pallas_call(
        functools.partial(self_heads_kernel, group),
        in_specs=[IN_HBM] * 4,
        out_specs=IN_HBM,
        out_shape=jax.ShapeDtypeStruct((heads, total, HD), BF16),
        scratch_shapes=[
            pltpu.VMEM((3, rows, width), BF16),
            pltpu.VMEM((owned, features), BF16),
            pltpu.VMEM((heads, total, HD), BF16),
            pltpu.SemaphoreType.DMA((3, heads // group)),
            pltpu.SemaphoreType.DMA,
            pltpu.SemaphoreType.DMA((heads // group,)),
        ],
        compiler_params=kernel_params(60),
        cost_estimate=pl.CostEstimate(
            flops=0, bytes_accessed=7 * rows * width * 2, transcendentals=0
        ),
        name="self_heads",
    )(q_local, k_local, v_local, audio)


def cross_heads_kernel(group, ids_ref, counts_ref, first_ref, q_ref, grad_ref, out_ref):
    rows = q_ref.shape[0]
    frames, slots = ids_ref.shape
    blocks = first_ref[0] + lax.broadcasted_iota(jnp.int32, (PAD, HD), 1) // AB
    row = lax.broadcasted_iota(jnp.int32, (PAD, HD), 0)
    live = jnp.zeros((PAD, HD), F32)
    for frame in range(frames):
        for slot in range(slots):
            hit = (blocks == ids_ref[frame, slot]) & (row == frame)
            hit = hit & (counts_ref[frame] > slot)
            live = jnp.where(hit, 1.0, live)
    live = live.astype(BF16)
    for head in range(group):
        cols = slice(head * HD, (head + 1) * HD)
        out_ref[head, 0:rows] = q_ref[:, cols]
        out_ref[head, rows : 2 * rows] = grad_ref[:, cols]
        out_ref[head, 2 * rows :] = live


def cross_heads(window_ids, live_counts, band_first, queries, grads):
    _, rows, width = queries.shape
    heads = width // HD
    group = 8
    total = 2 * rows + PAD
    block = pl.BlockSpec((None, rows, group * HD), lambda i: (0, 0, i))
    scalars = pl.BlockSpec(memory_space=pltpu.SMEM)
    return pl.pallas_call(
        functools.partial(cross_heads_kernel, group),
        grid=(heads // group,),
        in_specs=[scalars, scalars, scalars, block, block],
        out_specs=pl.BlockSpec((group, total, HD), lambda i: (i, 0, 0)),
        out_shape=jax.ShapeDtypeStruct((heads, total, HD), BF16),
        compiler_params=kernel_params(60),
        cost_estimate=pl.CostEstimate(
            flops=0, bytes_accessed=4 * rows * width * 2, transcendentals=0
        ),
        name="cross_heads",
    )(window_ids, live_counts, band_first, queries, grads)


def project_kernel(
    audio_first, place_ref, qkv_ref, other_ref, proj_ref, keys_ref, values_ref, audio, sem
):
    sources, owned, features = audio.shape
    chunks = features // HD // 2
    length = sources * owned
    edge = REACH * AB
    copies = []
    for chunk in range(chunks):
        for kind, (ref, first) in enumerate(((qkv_ref, audio_first), (other_ref, 0))):
            lanes = pl.ds(pl.multiple_of(place_ref[kind] + chunk * HD, HD), HD)
            copies.append(
                pltpu.make_async_copy(
                    ref.at[:, pl.ds(first + chunk * owned, owned), :],
                    audio.at[:, :, lanes],
                    sem.at[kind, chunk],
                )
            )
            copies[-1].start()
    tail = keys_ref.shape[0] - edge - length
    for ref in (keys_ref, values_ref):
        ref[0:edge] = jnp.zeros((edge, HD), BF16)
        ref[edge + length :] = jnp.zeros((tail, HD), BF16)
    for copy in copies:
        copy.wait()
    step = 256
    per = step // owned
    for i in range(length // step):
        rows = audio[i * per : (i + 1) * per].reshape(step, features)
        both = jnp.dot(rows, proj_ref[...], preferred_element_type=F32).astype(BF16)
        keys_ref[edge + i * step : edge + (i + 1) * step] = both[:, :HD]
        values_ref[edge + i * step : edge + (i + 1) * step] = both[:, HD:]


def projected(place, qkv, audio_first, other, proj):
    sources, audio_rows, _ = other.shape
    features = proj.shape[0]
    owned = 2 * AB
    length = sources * owned
    padded = length + HD - owned
    anywhere = pl.BlockSpec(memory_space=pl.ANY)
    flat = pl.BlockSpec((padded, HD), lambda i: (0, 0))
    return pl.pallas_call(
        functools.partial(project_kernel, audio_first),
        grid=(1,),
        in_specs=[
            pl.BlockSpec(memory_space=pltpu.SMEM),
            anywhere,
            anywhere,
            pl.BlockSpec((features, 2 * HD), lambda i: (0, 0)),
        ],
        out_specs=[flat, flat],
        out_shape=[jax.ShapeDtypeStruct((padded, HD), BF16)] * 2,
        scratch_shapes=[
            pltpu.VMEM((sources, owned, features), BF16),
            pltpu.SemaphoreType.DMA((2, features // HD // 2)),
        ],
        compiler_params=kernel_params(16),
        cost_estimate=pl.CostEstimate(
            flops=4 * length * features * HD,
            bytes_accessed=2 * (length * features + proj.size + 2 * padded * HD),
            transcendentals=0,
        ),
        name="projected",
    )(place, qkv, other, proj)


def cross_kernel(
    rows,
    place_ref,
    got,
    own,
    keys_ref,
    values_ref,
    proj_ref,
    out,
    terms,
    away,
    d_keys,
    d_values,
):
    sources = got.shape[0]
    owned = AB * 2
    features = proj_ref.shape[0]
    half = features // 2
    chunks = half // HD
    length = sources * owned
    edge = REACH * AB
    band = HD
    at_once = 16
    blocks = sources // at_once

    d_keys[...] = jnp.zeros_like(d_keys)
    d_values[...] = jnp.zeros_like(d_values)

    for block in range(blocks):
        sources_here = [block * at_once + i for i in range(at_once)]
        bands = [slice(t * owned, t * owned + band) for t in sources_here]
        k = [keys_ref[b] for b in bands]
        v = [values_ref[b] for b in bands]
        scores = [contract(got[t, 0:rows], k[i], 1, 1) for i, t in enumerate(sources_here)]
        d_probs = [
            contract(got[t, rows : 2 * rows], v[i], 1, 1) for i, t in enumerate(sources_here)
        ]
        weights = []
        for i, t in enumerate(sources_here):
            masks = got[t, 2 * rows :].astype(F32)
            live = jnp.concatenate(
                [jnp.broadcast_to(masks[f : f + 1], (rows // 2, band)) for f in range(2)], axis=0
            )
            masked = jnp.where(live > 0, scores[i], -1e30)
            top = jnp.max(masked, axis=1, keepdims=True)
            raised = jnp.exp2((masked - top) * EXP2_SCALING)
            weights.append(raised / jnp.sum(raised, axis=1, keepdims=True))
        weights_b = [part.astype(BF16) for part in weights]
        d_scores = []
        for i in range(at_once):
            weighed = weights[i] * d_probs[i]
            inner = jnp.sum(weighed, axis=1, keepdims=True)
            d_scores.append((weighed - weights[i] * inner).astype(BF16))
        for i, t in enumerate(sources_here):
            mixed = jnp.dot(weights_b[i], v[i], preferred_element_type=F32)
            out[t, 0:rows] = (own[t].astype(F32) + mixed).astype(BF16)
        for i, t in enumerate(sources_here):
            d_values[bands[i]] += contract(weights_b[i], got[t, rows : 2 * rows], 0, 0)
            d_keys[bands[i]] += contract(d_scores[i], got[t, 0:rows], 0, 0)

    own_proj = proj_ref[pl.ds(pl.multiple_of(place_ref[0], HD), half)]
    other_proj = proj_ref[pl.ds(pl.multiple_of(place_ref[1], HD), half)]
    step = length // blocks
    per = step // owned
    for block in range(blocks):
        rows_here = slice(edge + block * step, edge + (block + 1) * step)
        d_both = jnp.concatenate(
            [(d_keys[rows_here] * SCALING).astype(BF16), d_values[rows_here].astype(BF16)], axis=1
        )
        for buffer, part in ((away, other_proj), (terms, own_proj)):
            term = contract(d_both, part, 1, 1).astype(BF16)
            for chunk in range(chunks):
                buffer[
                    block * per : (block + 1) * per, chunk * owned : (chunk + 1) * owned
                ] = term[:, chunk * HD : (chunk + 1) * HD].reshape(per, owned, HD)


def cross_attention(place, got, own_heads, keys, values, proj):
    sources, rows, _ = own_heads.shape
    features = proj.shape[0]
    owned = 2 * AB
    padded = keys.shape[0]
    term_rows = features // 2 // HD * owned
    terms = jax.ShapeDtypeStruct((sources, term_rows, HD), BF16)

    def whole(array):
        return pl.BlockSpec(array.shape, lambda i: (0,) * len(array.shape))

    operands = (got, own_heads, keys, values, proj)
    results = [jax.ShapeDtypeStruct((sources, rows + term_rows, HD), BF16), terms, terms]
    return pl.pallas_call(
        functools.partial(cross_kernel, rows),
        grid=(1,),
        in_specs=[pl.BlockSpec(memory_space=pltpu.SMEM)] + [whole(x) for x in operands],
        out_specs=[whole(x) for x in results],
        out_shape=results,
        scratch_shapes=[pltpu.VMEM((padded, HD), F32), pltpu.VMEM((padded, HD), F32)],
        compiler_params=kernel_params(48),
        cost_estimate=pl.CostEstimate(
            flops=4 * sources * owned * features * HD + 10 * sources * rows * HD * HD,
            bytes_accessed=2 * (got.size + proj.size + 4 * own_heads.size),
            transcendentals=sources * rows * HD,
        ),
        name="cross_attention",
    )(place, *operands)


def self_attention_kernel(
    block_rows,
    block_keys,
    unrolled,
    q_ref,
    k_ref,
    v_ref,
    out_ref,
    keys_t,
    values_x,
    scores,
    tops,
):
    chunk = q_ref.shape[1]
    length = k_ref.shape[0] * chunk
    key_blocks = length // block_keys
    query_blocks = length // block_rows
    for piece in range(length // chunk):
        keys_t[:, piece * chunk : (piece + 1) * chunk] = k_ref[piece].T
        values_x[piece * chunk : (piece + 1) * chunk, :HD] = v_ref[piece]
    values_x[:, HD:] = jnp.ones((length, HD), BF16)
    per_block = block_rows // chunk

    def queries_of(block):
        rows = q_ref[pl.ds(block * per_block, per_block)]
        return rows.reshape(block_rows, HD)

    def highest(top, part):
        for group in range(part.shape[1] // HD):
            lanes = part[:, group * HD : (group + 1) * HD]
            top = lanes if top is None else jnp.maximum(top, lanes)
        return top

    def row_max(top):
        return jnp.broadcast_to(jnp.max(top, axis=1, keepdims=True), (block_rows, HD))

    first = queries_of(0)
    top = None
    for j in range(key_blocks):
        keys = slice(j * block_keys, (j + 1) * block_keys)
        part = jnp.dot(first, keys_t[:, keys], preferred_element_type=F32)
        scores[0, :, keys] = part
        top = highest(top, part)
    tops[0] = row_max(top)

    def one(block, slot, later):
        queries = queries_of(jnp.minimum(block + 1, query_blocks - 1))
        top_here = tops[slot][:, :1]
        top = None
        total = None
        for j in range(key_blocks):
            keys = slice(j * block_keys, (j + 1) * block_keys)
            part = jnp.dot(queries, keys_t[:, keys], preferred_element_type=F32)
            scores[later, :, keys] = part
            top = highest(top, part)
            raised = jnp.exp2((scores[slot, :, keys] - top_here) * EXP2_SCALING).astype(BF16)
            mixed = jnp.dot(raised, values_x[keys, :], preferred_element_type=F32)
            total = mixed if total is None else total + mixed
        tops[later] = row_max(top)
        own = (total[:, :HD] / total[:, HD:]).astype(BF16)
        out_ref[pl.ds(block * per_block, per_block)] = own.reshape(per_block, chunk, HD)

    def body(i, carry):
        for u in range(unrolled):
            one(i * unrolled + u, u % 2, 1 - u % 2)
        return carry

    lax.fori_loop(0, query_blocks // unrolled, body, 0)


def attend_self(qkv, rows):
    sources = qkv.shape[0]
    length = sources * rows
    block_rows, block_keys, unrolled = 512, 512, 4

    def whole(which):
        return pl.BlockSpec((sources, rows, HD), lambda i: (0, which, 0))

    flat = pl.BlockSpec((sources, rows, HD), lambda i: (0, 0, 0))
    return pl.pallas_call(
        functools.partial(self_attention_kernel, block_rows, block_keys, unrolled),
        grid=(1,),
        in_specs=[whole(0), whole(1), whole(2)],
        out_specs=flat,
        out_shape=jax.ShapeDtypeStruct((sources, rows, HD), BF16),
        scratch_shapes=[
            pltpu.VMEM((HD, length), BF16),
            pltpu.VMEM((length, 2 * HD), BF16),
            pltpu.VMEM((2, block_rows, length), F32),
            pltpu.VMEM((2, block_rows, HD), F32),
        ],
        compiler_params=kernel_params(48),
        cost_estimate=pl.CostEstimate(
            flops=8 * length * length * HD,
            bytes_accessed=8 * length * HD,
            transcendentals=length * length,
        ),
        name="self_attention",
    )(qkv, qkv, qkv)


def arrive_kernel(group, owned, got_ref, out_ref, sum_ref, total):
    rows = out_ref.shape[0]
    for head in range(group):
        out_ref[:, head * HD : (head + 1) * HD] = got_ref[head, 0:rows]

    @pl.when(pl.program_id(0) == 0)
    def _():
        total[...] = jnp.zeros_like(total)

    chunks = total.shape[1] // owned
    for core in range(2):
        part = total[core]
        for head in range(core, group, 2):
            part = part + got_ref[head, rows:].astype(F32)
        total[core] = part

    @pl.when(pl.program_id(0) == pl.num_programs(0) - 1)
    def _():
        for core in range(2):
            for chunk in range(chunks):
                lane = (core * chunks + chunk) * HD
                sum_ref[:, lane : lane + HD] = total[core, chunk * owned : (chunk + 1) * owned]


def arrived(got, rows, owned):
    heads, total, _ = got.shape
    features = 2 * (total - rows) // owned * HD
    group = 16
    return pl.pallas_call(
        functools.partial(arrive_kernel, group, owned),
        grid=(heads // group,),
        in_specs=[pl.BlockSpec((group, total, HD), lambda i: (i, 0, 0))],
        out_specs=[
            pl.BlockSpec((None, rows, group * HD), lambda i: (0, 0, i)),
            pl.BlockSpec((None, owned, features), lambda i: (0, 0, 0)),
        ],
        out_shape=[
            jax.ShapeDtypeStruct((1, rows, heads * HD), BF16),
            jax.ShapeDtypeStruct((1, owned, features), F32),
        ],
        scratch_shapes=[pltpu.VMEM((2, total - rows, HD), F32)],
        compiler_params=kernel_params(16),
        cost_estimate=pl.CostEstimate(
            flops=got.size, bytes_accessed=4 * got.size, transcendentals=0
        ),
        name="arrived",
    )(got)


def local(
    self_q,
    self_k,
    self_v,
    cross_q,
    audio,
    key_weight,
    value_weight,
    intersection,
    counts,
    cotangent,
):
    here = lax.axis_index("seq")
    core = lax.rem(here, 2)
    rows = self_q.shape[1]
    owned, features = audio.shape[1:]

    qkv = self_heads(self_q, self_k, self_v, audio)
    qkv, cross_q, key_weight, value_weight = lax.optimization_barrier(
        (qkv, cross_q, key_weight, value_weight)
    )
    qkv = handed_over(qkv)

    band_first = (here * (owned // AB) - REACH)[None].astype(jnp.int32)
    cross = cross_heads(intersection[0], counts[0], band_first, cross_q, cotangent)
    both = jnp.concatenate([key_weight, value_weight], axis=1)
    proj = gathered_by_doubling(both[None], "fsdp").reshape(-1, 2 * HD)
    place = jnp.stack([core, 1 - core]).astype(jnp.int32) * (features // 2)
    qkv, cross, proj, place = lax.optimization_barrier((qkv, cross, proj, place))

    cross = handed_over(cross)
    other = from_other_core(qkv[:, 3 * rows :])
    own_heads = attend_self(qkv, rows)
    keys, values = projected(place, qkv, 3 * rows, other, proj)
    sent, terms, away = cross_attention(place, cross, own_heads, keys, values, proj)
    both_terms = terms.astype(F32) + from_other_core(away).astype(F32)
    sent = lax.dynamic_update_slice(sent, both_terms.astype(BF16), (0, rows, 0))
    block_out, audio_grad = arrived(handed_over(sent), rows, owned)
    return (block_out, audio_grad)


def solution(mesh):
    in_specs = (
        P("fsdp", "seq", None),
        P("fsdp", "seq", None),
        P("fsdp", "seq", None),
        P("fsdp", "seq", None),
        P("fsdp", "seq", None),
        P("fsdp", "seq"),
        P("fsdp", "seq"),
        P("fsdp", "seq", None),
        P("fsdp", "seq"),
        P("fsdp", "seq", None),
    )
    out_specs = (P("fsdp", "seq", None), P("fsdp", "seq", None))
    return jax.shard_map(local, mesh=mesh, in_specs=in_specs, out_specs=out_specs, check_vma=False)
```

```python
import functools

import jax
import jax.numpy as jnp
from jax import lax
from jax.experimental import pallas as pl
from jax.experimental.pallas import tpu as pltpu
from jax.sharding import PartitionSpec as P

HD = 128
AB = 16
REACH = 3
PAD = 16
SCALING = HD ** (-0.5)
EXP2_SCALING = SCALING * 1.4426950408889634
F32 = jnp.float32
BF16 = jnp.bfloat16
MIB = 1024 * 1024


IN_HBM = pl.BlockSpec(memory_space=pltpu.HBM)


def kernel_params(mib=48):
    return pltpu.CompilerParams(vmem_limit_bytes=mib * MIB)


def handed_over(parts):
    return lax.all_to_all(parts, "seq", split_axis=0, concat_axis=0, tiled=True)


def gathered_by_doubling(block, axis):
    size = lax.axis_size(axis)
    here = lax.axis_index(axis)
    step = 1
    while step < size:
        other = lax.ppermute(block, axis, [(i, i ^ step) for i in range(size)])
        upper = (here & step) != 0
        block = jnp.concatenate(
            [jnp.where(upper, other, block), jnp.where(upper, block, other)], axis=0
        )
        step *= 2
    return block


def from_other_core(block):
    size = lax.axis_size("seq")
    return lax.ppermute(block, "seq", [(i, i ^ 1) for i in range(size)])


def contract(a, b, dim_a, dim_b):
    return lax.dot_general(a, b, (((dim_a,), (dim_b,)), ((), ())), preferred_element_type=F32)


def self_heads_kernel(
    group, q_hbm, k_hbm, v_hbm, audio_hbm, out_hbm, loaded, audio, out, in_sem, audio_sem, out_sem
):
    heads = out.shape[0]
    rows = loaded.shape[1]
    owned, features = audio.shape
    chunks = features // HD // 2
    loads = []
    for first in range(0, heads, group):
        cols = pl.ds(first * HD, group * HD)
        part = [
            pltpu.make_async_copy(
                source.at[0, :, cols], loaded.at[which, :, cols], in_sem.at[which, first // group]
            )
            for which, source in enumerate((q_hbm, k_hbm, v_hbm))
        ]
        for copy in part:
            copy.start()
        loads.append(part)
    audio_load = pltpu.make_async_copy(audio_hbm.at[0], audio, audio_sem)
    audio_load.start()
    audio_load.wait()
    stores = []
    for part in range(len(loads)):
        for copy in loads[part]:
            copy.wait()
        for head in range(part * group, (part + 1) * group):
            for which in range(3):
                out[head, which * rows : (which + 1) * rows] = loaded[
                    which, :, head * HD : (head + 1) * HD
                ]
            for chunk in range(chunks):
                first = 3 * rows + chunk * owned
                lane = (head % 2 * chunks + chunk) * HD
                out[head, first : first + owned] = audio[:, lane : lane + HD]
        here = pl.ds(part * group, group)
        stores.append(pltpu.make_async_copy(out.at[here], out_hbm.at[here], out_sem.at[part]))
        stores[-1].start()
    for copy in stores:
        copy.wait()


def self_heads(q_local, k_local, v_local, audio):
    _, rows, width = q_local.shape
    _, owned, features = audio.shape
    heads = width // HD
    group = 8
    total = 3 * rows + owned * (features // HD // 2)
    return pl.pallas_call(
        functools.partial(self_heads_kernel, group),
        in_specs=[IN_HBM] * 4,
        out_specs=IN_HBM,
        out_shape=jax.ShapeDtypeStruct((heads, total, HD), BF16),
        scratch_shapes=[
            pltpu.VMEM((3, rows, width), BF16),
            pltpu.VMEM((owned, features), BF16),
            pltpu.VMEM((heads, total, HD), BF16),
            pltpu.SemaphoreType.DMA((3, heads // group)),
            pltpu.SemaphoreType.DMA,
            pltpu.SemaphoreType.DMA((heads // group,)),
        ],
        compiler_params=kernel_params(60),
        cost_estimate=pl.CostEstimate(
            flops=0, bytes_accessed=7 * rows * width * 2, transcendentals=0
        ),
        name="self_heads",
    )(q_local, k_local, v_local, audio)


def cross_heads_kernel(group, ids_ref, counts_ref, first_ref, q_ref, grad_ref, out_ref):
    rows = q_ref.shape[0]
    frames, slots = ids_ref.shape
    blocks = first_ref[0] + lax.broadcasted_iota(jnp.int32, (PAD, HD), 1) // AB
    row = lax.broadcasted_iota(jnp.int32, (PAD, HD), 0)
    live = jnp.zeros((PAD, HD), F32)
    for frame in range(frames):
        for slot in range(slots):
            hit = (blocks == ids_ref[frame, slot]) & (row == frame)
            hit = hit & (counts_ref[frame] > slot)
            live = jnp.where(hit, 1.0, live)
    live = live.astype(BF16)
    for head in range(group):
        cols = slice(head * HD, (head + 1) * HD)
        out_ref[head, 0:rows] = q_ref[:, cols]
        out_ref[head, rows : 2 * rows] = grad_ref[:, cols]
        out_ref[head, 2 * rows :] = live


def cross_heads(window_ids, live_counts, band_first, queries, grads):
    _, rows, width = queries.shape
    heads = width // HD
    group = 8
    total = 2 * rows + PAD
    block = pl.BlockSpec((None, rows, group * HD), lambda i: (0, 0, i))
    scalars = pl.BlockSpec(memory_space=pltpu.SMEM)
    return pl.pallas_call(
        functools.partial(cross_heads_kernel, group),
        grid=(heads // group,),
        in_specs=[scalars, scalars, scalars, block, block],
        out_specs=pl.BlockSpec((group, total, HD), lambda i: (i, 0, 0)),
        out_shape=jax.ShapeDtypeStruct((heads, total, HD), BF16),
        compiler_params=kernel_params(60),
        cost_estimate=pl.CostEstimate(
            flops=0, bytes_accessed=4 * rows * width * 2, transcendentals=0
        ),
        name="cross_heads",
    )(window_ids, live_counts, band_first, queries, grads)


def project_kernel(
    audio_first, place_ref, qkv_ref, other_ref, proj_ref, keys_ref, values_ref, audio, sem
):
    sources, owned, features = audio.shape
    chunks = features // HD // 2
    length = sources * owned
    edge = REACH * AB
    copies = []
    for chunk in range(chunks):
        for kind, (ref, first) in enumerate(((qkv_ref, audio_first), (other_ref, 0))):
            lanes = pl.ds(pl.multiple_of(place_ref[kind] + chunk * HD, HD), HD)
            copies.append(
                pltpu.make_async_copy(
                    ref.at[:, pl.ds(first + chunk * owned, owned), :],
                    audio.at[:, :, lanes],
                    sem.at[kind, chunk],
                )
            )
            copies[-1].start()
    tail = keys_ref.shape[0] - edge - length
    for ref in (keys_ref, values_ref):
        ref[0:edge] = jnp.zeros((edge, HD), BF16)
        ref[edge + length :] = jnp.zeros((tail, HD), BF16)
    for copy in copies:
        copy.wait()
    step = 256
    per = step // owned
    for i in range(length // step):
        rows = audio[i * per : (i + 1) * per].reshape(step, features)
        both = jnp.dot(rows, proj_ref[...], preferred_element_type=F32).astype(BF16)
        keys_ref[edge + i * step : edge + (i + 1) * step] = both[:, :HD]
        values_ref[edge + i * step : edge + (i + 1) * step] = both[:, HD:]


def projected(place, qkv, audio_first, other, proj):
    sources, audio_rows, _ = other.shape
    features = proj.shape[0]
    owned = 2 * AB
    length = sources * owned
    padded = length + HD - owned
    anywhere = pl.BlockSpec(memory_space=pl.ANY)
    flat = pl.BlockSpec((padded, HD), lambda i: (0, 0))
    return pl.pallas_call(
        functools.partial(project_kernel, audio_first),
        grid=(1,),
        in_specs=[
            pl.BlockSpec(memory_space=pltpu.SMEM),
            anywhere,
            anywhere,
            pl.BlockSpec((features, 2 * HD), lambda i: (0, 0)),
        ],
        out_specs=[flat, flat],
        out_shape=[jax.ShapeDtypeStruct((padded, HD), BF16)] * 2,
        scratch_shapes=[
            pltpu.VMEM((sources, owned, features), BF16),
            pltpu.SemaphoreType.DMA((2, features // HD // 2)),
        ],
        compiler_params=kernel_params(16),
        cost_estimate=pl.CostEstimate(
            flops=4 * length * features * HD,
            bytes_accessed=2 * (length * features + proj.size + 2 * padded * HD),
            transcendentals=0,
        ),
        name="projected",
    )(place, qkv, other, proj)


def cross_kernel(
    rows,
    place_ref,
    got,
    own,
    keys_ref,
    values_ref,
    proj_ref,
    out,
    terms,
    away,
    d_keys,
    d_values,
):
    sources = got.shape[0]
    owned = AB * 2
    features = proj_ref.shape[0]
    half = features // 2
    chunks = half // HD
    length = sources * owned
    edge = REACH * AB
    band = HD
    at_once = 16
    blocks = sources // at_once

    d_keys[...] = jnp.zeros_like(d_keys)
    d_values[...] = jnp.zeros_like(d_values)

    for block in range(blocks):
        sources_here = [block * at_once + i for i in range(at_once)]
        bands = [slice(t * owned, t * owned + band) for t in sources_here]
        k = [keys_ref[b] for b in bands]
        v = [values_ref[b] for b in bands]
        scores = [contract(got[t, 0:rows], k[i], 1, 1) for i, t in enumerate(sources_here)]
        d_probs = [
            contract(got[t, rows : 2 * rows], v[i], 1, 1) for i, t in enumerate(sources_here)
        ]
        weights = []
        for i, t in enumerate(sources_here):
            masks = got[t, 2 * rows :].astype(F32)
            live = jnp.concatenate(
                [jnp.broadcast_to(masks[f : f + 1], (rows // 2, band)) for f in range(2)], axis=0
            )
            masked = jnp.where(live > 0, scores[i], -1e30)
            top = jnp.max(masked, axis=1, keepdims=True)
            raised = jnp.exp2((masked - top) * EXP2_SCALING)
            weights.append(raised / jnp.sum(raised, axis=1, keepdims=True))
        weights_b = [part.astype(BF16) for part in weights]
        d_scores = []
        for i in range(at_once):
            weighed = weights[i] * d_probs[i]
            inner = jnp.sum(weighed, axis=1, keepdims=True)
            d_scores.append((weighed - weights[i] * inner).astype(BF16))
        for i, t in enumerate(sources_here):
            mixed = jnp.dot(weights_b[i], v[i], preferred_element_type=F32)
            out[t, 0:rows] = (own[t].astype(F32) + mixed).astype(BF16)
        for i, t in enumerate(sources_here):
            d_values[bands[i]] += contract(weights_b[i], got[t, rows : 2 * rows], 0, 0)
            d_keys[bands[i]] += contract(d_scores[i], got[t, 0:rows], 0, 0)

    own_proj = proj_ref[pl.ds(pl.multiple_of(place_ref[0], HD), half)]
    other_proj = proj_ref[pl.ds(pl.multiple_of(place_ref[1], HD), half)]
    step = length // blocks
    per = step // owned
    for block in range(blocks):
        rows_here = slice(edge + block * step, edge + (block + 1) * step)
        d_both = jnp.concatenate(
            [(d_keys[rows_here] * SCALING).astype(BF16), d_values[rows_here].astype(BF16)], axis=1
        )
        for buffer, part in ((away, other_proj), (terms, own_proj)):
            term = contract(d_both, part, 1, 1).astype(BF16)
            for chunk in range(chunks):
                buffer[
                    block * per : (block + 1) * per, chunk * owned : (chunk + 1) * owned
                ] = term[:, chunk * HD : (chunk + 1) * HD].reshape(per, owned, HD)


def cross_attention(place, got, own_heads, keys, values, proj):
    sources, rows, _ = own_heads.shape
    features = proj.shape[0]
    owned = 2 * AB
    padded = keys.shape[0]
    term_rows = features // 2 // HD * owned
    terms = jax.ShapeDtypeStruct((sources, term_rows, HD), BF16)

    def whole(array):
        return pl.BlockSpec(array.shape, lambda i: (0,) * len(array.shape))

    operands = (got, own_heads, keys, values, proj)
    results = [jax.ShapeDtypeStruct((sources, rows + term_rows, HD), BF16), terms, terms]
    return pl.pallas_call(
        functools.partial(cross_kernel, rows),
        grid=(1,),
        in_specs=[pl.BlockSpec(memory_space=pltpu.SMEM)] + [whole(x) for x in operands],
        out_specs=[whole(x) for x in results],
        out_shape=results,
        scratch_shapes=[pltpu.VMEM((padded, HD), F32), pltpu.VMEM((padded, HD), F32)],
        compiler_params=kernel_params(40),
        cost_estimate=pl.CostEstimate(
            flops=4 * sources * owned * features * HD + 10 * sources * rows * HD * HD,
            bytes_accessed=2 * (got.size + proj.size + 4 * own_heads.size),
            transcendentals=sources * rows * HD,
        ),
        name="cross_attention",
    )(place, *operands)


def self_attention_kernel(
    block_rows,
    block_keys,
    unrolled,
    q_ref,
    k_ref,
    v_ref,
    out_ref,
    keys_t,
    values_x,
    scores,
    tops,
):
    chunk = q_ref.shape[1]
    length = k_ref.shape[0] * chunk
    key_blocks = length // block_keys
    query_blocks = length // block_rows
    for piece in range(length // chunk):
        keys_t[:, piece * chunk : (piece + 1) * chunk] = k_ref[piece].T
        values_x[piece * chunk : (piece + 1) * chunk, :HD] = v_ref[piece]
    values_x[:, HD:] = jnp.ones((length, HD), BF16)
    per_block = block_rows // chunk

    def queries_of(block):
        rows = q_ref[pl.ds(block * per_block, per_block)]
        return rows.reshape(block_rows, HD)

    def highest(top, part):
        for group in range(part.shape[1] // HD):
            lanes = part[:, group * HD : (group + 1) * HD]
            top = lanes if top is None else jnp.maximum(top, lanes)
        return top

    def row_max(top):
        return jnp.broadcast_to(jnp.max(top, axis=1, keepdims=True), (block_rows, HD))

    first = queries_of(0)
    top = None
    for j in range(key_blocks):
        keys = slice(j * block_keys, (j + 1) * block_keys)
        part = jnp.dot(first, keys_t[:, keys], preferred_element_type=F32)
        scores[0, :, keys] = part
        top = highest(top, part)
    tops[0] = row_max(top)

    def one(block, slot, later):
        queries = queries_of(jnp.minimum(block + 1, query_blocks - 1))
        top_here = tops[slot][:, :1]
        top = None
        total = None
        for j in range(key_blocks):
            keys = slice(j * block_keys, (j + 1) * block_keys)
            part = jnp.dot(queries, keys_t[:, keys], preferred_element_type=F32)
            scores[later, :, keys] = part
            top = highest(top, part)
            raised = jnp.exp2((scores[slot, :, keys] - top_here) * EXP2_SCALING).astype(BF16)
            mixed = jnp.dot(raised, values_x[keys, :], preferred_element_type=F32)
            total = mixed if total is None else total + mixed
        tops[later] = row_max(top)
        own = (total[:, :HD] / total[:, HD:]).astype(BF16)
        out_ref[pl.ds(block * per_block, per_block)] = own.reshape(per_block, chunk, HD)

    def body(i, carry):
        for u in range(unrolled):
            one(i * unrolled + u, u % 2, 1 - u % 2)
        return carry

    lax.fori_loop(0, query_blocks // unrolled, body, 0)


def attend_self(qkv, rows):
    sources = qkv.shape[0]
    length = sources * rows
    block_rows, block_keys, unrolled = 512, 512, 4

    def whole(which):
        return pl.BlockSpec((sources, rows, HD), lambda i: (0, which, 0))

    flat = pl.BlockSpec((sources, rows, HD), lambda i: (0, 0, 0))
    return pl.pallas_call(
        functools.partial(self_attention_kernel, block_rows, block_keys, unrolled),
        grid=(1,),
        in_specs=[whole(0), whole(1), whole(2)],
        out_specs=flat,
        out_shape=jax.ShapeDtypeStruct((sources, rows, HD), BF16),
        scratch_shapes=[
            pltpu.VMEM((HD, length), BF16),
            pltpu.VMEM((length, 2 * HD), BF16),
            pltpu.VMEM((2, block_rows, length), F32),
            pltpu.VMEM((2, block_rows, HD), F32),
        ],
        compiler_params=kernel_params(48),
        cost_estimate=pl.CostEstimate(
            flops=8 * length * length * HD,
            bytes_accessed=8 * length * HD,
            transcendentals=length * length,
        ),
        name="self_attention",
    )(qkv, qkv, qkv)


def arrive_kernel(group, owned, got_ref, out_ref, sum_ref, total):
    rows = out_ref.shape[0]
    for head in range(group):
        out_ref[:, head * HD : (head + 1) * HD] = got_ref[head, 0:rows]

    @pl.when(pl.program_id(0) == 0)
    def _():
        total[...] = jnp.zeros_like(total)

    chunks = total.shape[1] // owned
    for core in range(2):
        part = total[core]
        for head in range(core, group, 2):
            part = part + got_ref[head, rows:].astype(F32)
        total[core] = part

    @pl.when(pl.program_id(0) == pl.num_programs(0) - 1)
    def _():
        for core in range(2):
            for chunk in range(chunks):
                lane = (core * chunks + chunk) * HD
                sum_ref[:, lane : lane + HD] = total[core, chunk * owned : (chunk + 1) * owned]


def arrived(got, rows, owned):
    heads, total, _ = got.shape
    features = 2 * (total - rows) // owned * HD
    group = 16
    return pl.pallas_call(
        functools.partial(arrive_kernel, group, owned),
        grid=(heads // group,),
        in_specs=[pl.BlockSpec((group, total, HD), lambda i: (i, 0, 0))],
        out_specs=[
            pl.BlockSpec((None, rows, group * HD), lambda i: (0, 0, i)),
            pl.BlockSpec((None, owned, features), lambda i: (0, 0, 0)),
        ],
        out_shape=[
            jax.ShapeDtypeStruct((1, rows, heads * HD), BF16),
            jax.ShapeDtypeStruct((1, owned, features), F32),
        ],
        scratch_shapes=[pltpu.VMEM((2, total - rows, HD), F32)],
        compiler_params=kernel_params(16),
        cost_estimate=pl.CostEstimate(
            flops=got.size, bytes_accessed=4 * got.size, transcendentals=0
        ),
        name="arrived",
    )(got)


def local(
    self_q,
    self_k,
    self_v,
    cross_q,
    audio,
    key_weight,
    value_weight,
    intersection,
    counts,
    cotangent,
):
    here = lax.axis_index("seq")
    core = lax.rem(here, 2)
    rows = self_q.shape[1]
    owned, features = audio.shape[1:]

    qkv = self_heads(self_q, self_k, self_v, audio)
    qkv, cross_q, key_weight, value_weight = lax.optimization_barrier(
        (qkv, cross_q, key_weight, value_weight)
    )
    qkv = handed_over(qkv)

    band_first = (here * (owned // AB) - REACH)[None].astype(jnp.int32)
    cross = cross_heads(intersection[0], counts[0], band_first, cross_q, cotangent)
    both = jnp.concatenate([key_weight, value_weight], axis=1)
    proj = gathered_by_doubling(both[None], "fsdp").reshape(-1, 2 * HD)
    place = jnp.stack([core, 1 - core]).astype(jnp.int32) * (features // 2)
    qkv, cross, proj, place = lax.optimization_barrier((qkv, cross, proj, place))

    cross = handed_over(cross)
    other = from_other_core(qkv[:, 3 * rows :])
    own_heads = attend_self(qkv, rows)
    keys, values = projected(place, qkv, 3 * rows, other, proj)
    sent, terms, away = cross_attention(place, cross, own_heads, keys, values, proj)
    both_terms = terms.astype(F32) + from_other_core(away).astype(F32)
    sent = lax.dynamic_update_slice(sent, both_terms.astype(BF16), (0, rows, 0))
    block_out, audio_grad = arrived(handed_over(sent), rows, owned)
    return (block_out, audio_grad)


def solution(mesh):
    in_specs = (
        P("fsdp", "seq", None),
        P("fsdp", "seq", None),
        P("fsdp", "seq", None),
        P("fsdp", "seq", None),
        P("fsdp", "seq", None),
        P("fsdp", "seq"),
        P("fsdp", "seq"),
        P("fsdp", "seq", None),
        P("fsdp", "seq"),
        P("fsdp", "seq", None),
    )
    out_specs = (P("fsdp", "seq", None), P("fsdp", "seq", None))
    return jax.shard_map(local, mesh=mesh, in_specs=in_specs, out_specs=out_specs, check_vma=False)
```

```python
import functools

import jax
import jax.numpy as jnp
from jax import lax
from jax.experimental import pallas as pl
from jax.experimental.pallas import tpu as pltpu
from jax.sharding import PartitionSpec as P

HD = 128
AB = 16
REACH = 3
PAD = 16
SCALING = HD ** (-0.5)
EXP2_SCALING = SCALING * 1.4426950408889634
F32 = jnp.float32
BF16 = jnp.bfloat16
MIB = 1024 * 1024


IN_HBM = pl.BlockSpec(memory_space=pltpu.HBM)


def kernel_params(mib=48):
    return pltpu.CompilerParams(vmem_limit_bytes=mib * MIB)


def handed_over(parts):
    return lax.all_to_all(parts, "seq", split_axis=0, concat_axis=0, tiled=True)


def gathered_by_doubling(block, axis):
    size = lax.axis_size(axis)
    here = lax.axis_index(axis)
    step = 1
    while step < size:
        other = lax.ppermute(block, axis, [(i, i ^ step) for i in range(size)])
        upper = (here & step) != 0
        block = jnp.concatenate(
            [jnp.where(upper, other, block), jnp.where(upper, block, other)], axis=0
        )
        step *= 2
    return block


def from_other_core(block):
    size = lax.axis_size("seq")
    return lax.ppermute(block, "seq", [(i, i ^ 1) for i in range(size)])


def contract(a, b, dim_a, dim_b):
    return lax.dot_general(a, b, (((dim_a,), (dim_b,)), ((), ())), preferred_element_type=F32)


def self_heads_kernel(
    group, q_hbm, k_hbm, v_hbm, audio_hbm, out_hbm, loaded, audio, out, in_sem, audio_sem, out_sem
):
    heads = out.shape[0]
    rows = loaded.shape[1]
    owned, features = audio.shape
    chunks = features // HD // 2
    audio_load = pltpu.make_async_copy(audio_hbm.at[0], audio, audio_sem)
    audio_load.start()
    loads = []
    for first in range(0, heads, group):
        cols = pl.ds(first * HD, group * HD)
        part = [
            pltpu.make_async_copy(
                source.at[0, :, cols], loaded.at[which, :, cols], in_sem.at[which, first // group]
            )
            for which, source in enumerate((q_hbm, k_hbm, v_hbm))
        ]
        for copy in part:
            copy.start()
        loads.append(part)
    audio_load.wait()
    stores = []
    for part in range(len(loads)):
        for copy in loads[part]:
            copy.wait()
        for head in range(part * group, (part + 1) * group):
            for which in range(3):
                out[head, which * rows : (which + 1) * rows] = loaded[
                    which, :, head * HD : (head + 1) * HD
                ]
            for chunk in range(chunks):
                first = 3 * rows + chunk * owned
                lane = (head % 2 * chunks + chunk) * HD
                out[head, first : first + owned] = audio[:, lane : lane + HD]
        here = pl.ds(part * group, group)
        stores.append(pltpu.make_async_copy(out.at[here], out_hbm.at[here], out_sem.at[part]))
        stores[-1].start()
    for copy in stores:
        copy.wait()


def self_heads(q_local, k_local, v_local, audio):
    _, rows, width = q_local.shape
    _, owned, features = audio.shape
    heads = width // HD
    group = 8
    total = 3 * rows + owned * (features // HD // 2)
    return pl.pallas_call(
        functools.partial(self_heads_kernel, group),
        in_specs=[IN_HBM] * 4,
        out_specs=IN_HBM,
        out_shape=jax.ShapeDtypeStruct((heads, total, HD), BF16),
        scratch_shapes=[
            pltpu.VMEM((3, rows, width), BF16),
            pltpu.VMEM((owned, features), BF16),
            pltpu.VMEM((heads, total, HD), BF16),
            pltpu.SemaphoreType.DMA((3, heads // group)),
            pltpu.SemaphoreType.DMA,
            pltpu.SemaphoreType.DMA((heads // group,)),
        ],
        compiler_params=kernel_params(60),
        cost_estimate=pl.CostEstimate(
            flops=0, bytes_accessed=7 * rows * width * 2, transcendentals=0
        ),
        name="self_heads",
    )(q_local, k_local, v_local, audio)


def cross_heads_kernel(group, ids_ref, counts_ref, first_ref, q_ref, grad_ref, out_ref):
    rows = q_ref.shape[0]
    frames, slots = ids_ref.shape
    blocks = first_ref[0] + lax.broadcasted_iota(jnp.int32, (PAD, HD), 1) // AB
    row = lax.broadcasted_iota(jnp.int32, (PAD, HD), 0)
    live = jnp.zeros((PAD, HD), F32)
    for frame in range(frames):
        for slot in range(slots):
            hit = (blocks == ids_ref[frame, slot]) & (row == frame)
            hit = hit & (counts_ref[frame] > slot)
            live = jnp.where(hit, 1.0, live)
    live = live.astype(BF16)
    for head in range(group):
        cols = slice(head * HD, (head + 1) * HD)
        out_ref[head, 0:rows] = q_ref[:, cols]
        out_ref[head, rows : 2 * rows] = grad_ref[:, cols]
        out_ref[head, 2 * rows :] = live


def cross_heads(window_ids, live_counts, band_first, queries, grads):
    _, rows, width = queries.shape
    heads = width // HD
    group = 8
    total = 2 * rows + PAD
    block = pl.BlockSpec((None, rows, group * HD), lambda i: (0, 0, i))
    scalars = pl.BlockSpec(memory_space=pltpu.SMEM)
    return pl.pallas_call(
        functools.partial(cross_heads_kernel, group),
        grid=(heads // group,),
        in_specs=[scalars, scalars, scalars, block, block],
        out_specs=pl.BlockSpec((group, total, HD), lambda i: (i, 0, 0)),
        out_shape=jax.ShapeDtypeStruct((heads, total, HD), BF16),
        compiler_params=kernel_params(60),
        cost_estimate=pl.CostEstimate(
            flops=0, bytes_accessed=4 * rows * width * 2, transcendentals=0
        ),
        name="cross_heads",
    )(window_ids, live_counts, band_first, queries, grads)


def project_kernel(
    audio_first, place_ref, qkv_ref, other_ref, proj_ref, keys_ref, values_ref, audio, sem
):
    sources, owned, features = audio.shape
    chunks = features // HD // 2
    length = sources * owned
    edge = REACH * AB
    copies = []
    for chunk in range(chunks):
        for kind, (ref, first) in enumerate(((qkv_ref, audio_first), (other_ref, 0))):
            lanes = pl.ds(pl.multiple_of(place_ref[kind] + chunk * HD, HD), HD)
            copies.append(
                pltpu.make_async_copy(
                    ref.at[:, pl.ds(first + chunk * owned, owned), :],
                    audio.at[:, :, lanes],
                    sem.at[kind, chunk],
                )
            )
            copies[-1].start()
    tail = keys_ref.shape[0] - edge - length
    for ref in (keys_ref, values_ref):
        ref[0:edge] = jnp.zeros((edge, HD), BF16)
        ref[edge + length :] = jnp.zeros((tail, HD), BF16)
    for copy in copies:
        copy.wait()
    step = 256
    per = step // owned
    for i in range(length // step):
        rows = audio[i * per : (i + 1) * per].reshape(step, features)
        both = jnp.dot(rows, proj_ref[...], preferred_element_type=F32).astype(BF16)
        keys_ref[edge + i * step : edge + (i + 1) * step] = both[:, :HD]
        values_ref[edge + i * step : edge + (i + 1) * step] = both[:, HD:]


def projected(place, qkv, audio_first, other, proj):
    sources, audio_rows, _ = other.shape
    features = proj.shape[0]
    owned = 2 * AB
    length = sources * owned
    padded = length + HD - owned
    anywhere = pl.BlockSpec(memory_space=pl.ANY)
    flat = pl.BlockSpec((padded, HD), lambda i: (0, 0))
    return pl.pallas_call(
        functools.partial(project_kernel, audio_first),
        grid=(1,),
        in_specs=[
            pl.BlockSpec(memory_space=pltpu.SMEM),
            anywhere,
            anywhere,
            pl.BlockSpec((features, 2 * HD), lambda i: (0, 0)),
        ],
        out_specs=[flat, flat],
        out_shape=[jax.ShapeDtypeStruct((padded, HD), BF16)] * 2,
        scratch_shapes=[
            pltpu.VMEM((sources, owned, features), BF16),
            pltpu.SemaphoreType.DMA((2, features // HD // 2)),
        ],
        compiler_params=kernel_params(16),
        cost_estimate=pl.CostEstimate(
            flops=4 * length * features * HD,
            bytes_accessed=2 * (length * features + proj.size + 2 * padded * HD),
            transcendentals=0,
        ),
        name="projected",
    )(place, qkv, other, proj)


def cross_kernel(
    rows,
    place_ref,
    got,
    own,
    keys_ref,
    values_ref,
    proj_ref,
    out,
    terms,
    away,
    d_keys,
    d_values,
):
    sources = got.shape[0]
    owned = AB * 2
    features = proj_ref.shape[0]
    half = features // 2
    chunks = half // HD
    length = sources * owned
    edge = REACH * AB
    band = HD
    at_once = 16
    blocks = sources // at_once

    d_keys[...] = jnp.zeros_like(d_keys)
    d_values[...] = jnp.zeros_like(d_values)

    for block in range(blocks):
        sources_here = [block * at_once + i for i in range(at_once)]
        bands = [slice(t * owned, t * owned + band) for t in sources_here]
        k = [keys_ref[b] for b in bands]
        v = [values_ref[b] for b in bands]
        scores = [contract(got[t, 0:rows], k[i], 1, 1) for i, t in enumerate(sources_here)]
        d_probs = [
            contract(got[t, rows : 2 * rows], v[i], 1, 1) for i, t in enumerate(sources_here)
        ]
        weights = []
        for i, t in enumerate(sources_here):
            masks = got[t, 2 * rows :].astype(F32)
            live = jnp.concatenate(
                [jnp.broadcast_to(masks[f : f + 1], (rows // 2, band)) for f in range(2)], axis=0
            )
            masked = jnp.where(live > 0, scores[i], -1e30)
            top = jnp.max(masked, axis=1, keepdims=True)
            raised = jnp.exp2((masked - top) * EXP2_SCALING)
            weights.append(raised / jnp.sum(raised, axis=1, keepdims=True))
        weights_b = [part.astype(BF16) for part in weights]
        d_scores = []
        for i in range(at_once):
            weighed = weights[i] * d_probs[i]
            inner = jnp.sum(weighed, axis=1, keepdims=True)
            d_scores.append((weighed - weights[i] * inner).astype(BF16))
        for i, t in enumerate(sources_here):
            mixed = jnp.dot(weights_b[i], v[i], preferred_element_type=F32)
            out[t, 0:rows] = (own[t].astype(F32) + mixed).astype(BF16)
        for i, t in enumerate(sources_here):
            d_values[bands[i]] += contract(weights_b[i], got[t, rows : 2 * rows], 0, 0)
            d_keys[bands[i]] += contract(d_scores[i], got[t, 0:rows], 0, 0)

    own_proj = proj_ref[pl.ds(pl.multiple_of(place_ref[0], HD), half)]
    other_proj = proj_ref[pl.ds(pl.multiple_of(place_ref[1], HD), half)]
    step = length // blocks
    per = step // owned
    for block in range(blocks):
        rows_here = slice(edge + block * step, edge + (block + 1) * step)
        d_both = jnp.concatenate(
            [(d_keys[rows_here] * SCALING).astype(BF16), d_values[rows_here].astype(BF16)], axis=1
        )
        for buffer, part in ((away, other_proj), (terms, own_proj)):
            term = contract(d_both, part, 1, 1).astype(BF16)
            for chunk in range(chunks):
                buffer[
                    block * per : (block + 1) * per, chunk * owned : (chunk + 1) * owned
                ] = term[:, chunk * HD : (chunk + 1) * HD].reshape(per, owned, HD)


def cross_attention(place, got, own_heads, keys, values, proj):
    sources, rows, _ = own_heads.shape
    features = proj.shape[0]
    owned = 2 * AB
    padded = keys.shape[0]
    term_rows = features // 2 // HD * owned
    terms = jax.ShapeDtypeStruct((sources, term_rows, HD), BF16)

    def whole(array):
        return pl.BlockSpec(array.shape, lambda i: (0,) * len(array.shape))

    operands = (got, own_heads, keys, values, proj)
    results = [jax.ShapeDtypeStruct((sources, rows + term_rows, HD), BF16), terms, terms]
    return pl.pallas_call(
        functools.partial(cross_kernel, rows),
        grid=(1,),
        in_specs=[pl.BlockSpec(memory_space=pltpu.SMEM)] + [whole(x) for x in operands],
        out_specs=[whole(x) for x in results],
        out_shape=results,
        scratch_shapes=[pltpu.VMEM((padded, HD), F32), pltpu.VMEM((padded, HD), F32)],
        compiler_params=kernel_params(40),
        cost_estimate=pl.CostEstimate(
            flops=4 * sources * owned * features * HD + 10 * sources * rows * HD * HD,
            bytes_accessed=2 * (got.size + proj.size + 4 * own_heads.size),
            transcendentals=sources * rows * HD,
        ),
        name="cross_attention",
    )(place, *operands)


def self_attention_kernel(
    block_rows,
    block_keys,
    unrolled,
    q_ref,
    k_ref,
    v_ref,
    out_ref,
    keys_t,
    values_x,
    scores,
    tops,
):
    chunk = q_ref.shape[1]
    length = k_ref.shape[0] * chunk
    key_blocks = length // block_keys
    query_blocks = length // block_rows
    for piece in range(length // chunk):
        keys_t[:, piece * chunk : (piece + 1) * chunk] = k_ref[piece].T
        values_x[piece * chunk : (piece + 1) * chunk, :HD] = v_ref[piece]
    values_x[:, HD:] = jnp.ones((length, HD), BF16)
    per_block = block_rows // chunk

    def queries_of(block):
        rows = q_ref[pl.ds(block * per_block, per_block)]
        return rows.reshape(block_rows, HD)

    def highest(top, part):
        for group in range(part.shape[1] // HD):
            lanes = part[:, group * HD : (group + 1) * HD]
            top = lanes if top is None else jnp.maximum(top, lanes)
        return top

    def row_max(top):
        return jnp.broadcast_to(jnp.max(top, axis=1, keepdims=True), (block_rows, HD))

    first = queries_of(0)
    top = None
    for j in range(key_blocks):
        keys = slice(j * block_keys, (j + 1) * block_keys)
        part = jnp.dot(first, keys_t[:, keys], preferred_element_type=F32)
        scores[0, :, keys] = part
        top = highest(top, part)
    tops[0] = row_max(top)

    def one(block, slot, later):
        queries = queries_of(jnp.minimum(block + 1, query_blocks - 1))
        top_here = tops[slot][:, :1]
        top = None
        total = None
        for j in range(key_blocks):
            keys = slice(j * block_keys, (j + 1) * block_keys)
            part = jnp.dot(queries, keys_t[:, keys], preferred_element_type=F32)
            scores[later, :, keys] = part
            top = highest(top, part)
            raised = jnp.exp2((scores[slot, :, keys] - top_here) * EXP2_SCALING).astype(BF16)
            mixed = jnp.dot(raised, values_x[keys, :], preferred_element_type=F32)
            total = mixed if total is None else total + mixed
        tops[later] = row_max(top)
        own = (total[:, :HD] / total[:, HD:]).astype(BF16)
        out_ref[pl.ds(block * per_block, per_block)] = own.reshape(per_block, chunk, HD)

    def body(i, carry):
        for u in range(unrolled):
            one(i * unrolled + u, u % 2, 1 - u % 2)
        return carry

    lax.fori_loop(0, query_blocks // unrolled, body, 0)


def attend_self(qkv, rows):
    sources = qkv.shape[0]
    length = sources * rows
    block_rows, block_keys, unrolled = 512, 512, 4

    def whole(which):
        return pl.BlockSpec((sources, rows, HD), lambda i: (0, which, 0))

    flat = pl.BlockSpec((sources, rows, HD), lambda i: (0, 0, 0))
    return pl.pallas_call(
        functools.partial(self_attention_kernel, block_rows, block_keys, unrolled),
        grid=(1,),
        in_specs=[whole(0), whole(1), whole(2)],
        out_specs=flat,
        out_shape=jax.ShapeDtypeStruct((sources, rows, HD), BF16),
        scratch_shapes=[
            pltpu.VMEM((HD, length), BF16),
            pltpu.VMEM((length, 2 * HD), BF16),
            pltpu.VMEM((2, block_rows, length), F32),
            pltpu.VMEM((2, block_rows, HD), F32),
        ],
        compiler_params=kernel_params(48),
        cost_estimate=pl.CostEstimate(
            flops=8 * length * length * HD,
            bytes_accessed=8 * length * HD,
            transcendentals=length * length,
        ),
        name="self_attention",
    )(qkv, qkv, qkv)


def arrive_kernel(group, owned, got_ref, out_ref, sum_ref, total):
    rows = out_ref.shape[0]
    for head in range(group):
        out_ref[:, head * HD : (head + 1) * HD] = got_ref[head, 0:rows]

    @pl.when(pl.program_id(0) == 0)
    def _():
        total[...] = jnp.zeros_like(total)

    chunks = total.shape[1] // owned
    for core in range(2):
        part = total[core]
        for head in range(core, group, 2):
            part = part + got_ref[head, rows:].astype(F32)
        total[core] = part

    @pl.when(pl.program_id(0) == pl.num_programs(0) - 1)
    def _():
        for core in range(2):
            for chunk in range(chunks):
                lane = (core * chunks + chunk) * HD
                sum_ref[:, lane : lane + HD] = total[core, chunk * owned : (chunk + 1) * owned]


def arrived(got, rows, owned):
    heads, total, _ = got.shape
    features = 2 * (total - rows) // owned * HD
    group = 16
    return pl.pallas_call(
        functools.partial(arrive_kernel, group, owned),
        grid=(heads // group,),
        in_specs=[pl.BlockSpec((group, total, HD), lambda i: (i, 0, 0))],
        out_specs=[
            pl.BlockSpec((None, rows, group * HD), lambda i: (0, 0, i)),
            pl.BlockSpec((None, owned, features), lambda i: (0, 0, 0)),
        ],
        out_shape=[
            jax.ShapeDtypeStruct((1, rows, heads * HD), BF16),
            jax.ShapeDtypeStruct((1, owned, features), F32),
        ],
        scratch_shapes=[pltpu.VMEM((2, total - rows, HD), F32)],
        compiler_params=kernel_params(16),
        cost_estimate=pl.CostEstimate(
            flops=got.size, bytes_accessed=4 * got.size, transcendentals=0
        ),
        name="arrived",
    )(got)


def local(
    self_q,
    self_k,
    self_v,
    cross_q,
    audio,
    key_weight,
    value_weight,
    intersection,
    counts,
    cotangent,
):
    here = lax.axis_index("seq")
    core = lax.rem(here, 2)
    rows = self_q.shape[1]
    owned, features = audio.shape[1:]

    qkv = self_heads(self_q, self_k, self_v, audio)
    qkv, cross_q, key_weight, value_weight = lax.optimization_barrier(
        (qkv, cross_q, key_weight, value_weight)
    )
    qkv = handed_over(qkv)

    band_first = (here * (owned // AB) - REACH)[None].astype(jnp.int32)
    cross = cross_heads(intersection[0], counts[0], band_first, cross_q, cotangent)
    both = jnp.concatenate([key_weight, value_weight], axis=1)
    proj = gathered_by_doubling(both[None], "fsdp").reshape(-1, 2 * HD)
    place = jnp.stack([core, 1 - core]).astype(jnp.int32) * (features // 2)
    qkv, cross, proj, place = lax.optimization_barrier((qkv, cross, proj, place))

    cross = handed_over(cross)
    other = from_other_core(qkv[:, 3 * rows :])
    own_heads = attend_self(qkv, rows)
    keys, values = projected(place, qkv, 3 * rows, other, proj)
    sent, terms, away = cross_attention(place, cross, own_heads, keys, values, proj)
    both_terms = terms.astype(F32) + from_other_core(away).astype(F32)
    sent = lax.dynamic_update_slice(sent, both_terms.astype(BF16), (0, rows, 0))
    block_out, audio_grad = arrived(handed_over(sent), rows, owned)
    return (block_out, audio_grad)


def solution(mesh):
    in_specs = (
        P("fsdp", "seq", None),
        P("fsdp", "seq", None),
        P("fsdp", "seq", None),
        P("fsdp", "seq", None),
        P("fsdp", "seq", None),
        P("fsdp", "seq"),
        P("fsdp", "seq"),
        P("fsdp", "seq", None),
        P("fsdp", "seq"),
        P("fsdp", "seq", None),
    )
    out_specs = (P("fsdp", "seq", None), P("fsdp", "seq", None))
    return jax.shard_map(local, mesh=mesh, in_specs=in_specs, out_specs=out_specs, check_vma=False)
```
